32 devices in a mesh: tm: 4 (over y, x), space: 4 (over z), ens: 2 (over core).
Axes of the slice: x: 2, y: 2, z: 4, core: 2. Of those that a mesh axis runs over, the one named last changes fastest.
Arguments:
- start_states: float32 [4, 16, 256, 1024], P('tm', 'ens', 'space'), may hold values from -6 to 6
- velocity_x: float32 [256, 1024], P('space'), may hold values from -0.15 to 0.15
- velocity_y: float32 [256, 1024], P('space'), may hold values from -0.15 to 0.15
- diffusivity: float32 [256, 1024], P('space'), may hold values from 0.06 to 0.2
- source_shape: float32 [256, 1024], P('space'), may hold values from -6 to 6
- params: float32 [16, 128], P('ens'), may hold values from -6 to 6
- obs_cell: int32 [4, 256], P('tm', 'space'), may hold values from 0 to 262143, as said below
- obs_data: float32 [4, 256], P('tm', 'space'), may hold values from -6 to 6
- obs_noise: float32 [4, 256, 16], P('tm', 'space'), may hold values from -6 to 6
- obs_var: float32 [4, 256], P('tm', 'space'), may hold values from 0.05 to 0.5
Outputs:
- new_states: float32 [4, 16, 256, 1024], P('tm', 'ens', 'space')
- new_params: float32 [16, 128], P('ens')
The draws below stay inside these ranges and needn't reach their ends.
Inputs may be any that keep to these rules, and one draw needn't show every extreme that they name: `obs_cell`: entry (n, o) lies in the rows of slab o // 64, that is row (o // 64) * 64 up to 63 rows further.
All inputs are finite; a program needn't handle non-finite values.
Results may differ from the reference program's by a relative error of at most 0.0003.
Values sent between devices are 32-bit elements; how exact they have to be, the bound alone decides.
A program may use at most 128 MiB of HBM per device.

```python
import math
import jax
import jax.numpy as jnp
from jax import lax

ROWS_DEV = 64
COLS = 1024
FINE = 4
PARAMS = 128
OBS_DEV = 64
SLICES = 4
MEMBERS = 16
NY = 256
OBS = 256
BAND = 8


def draw_obs_cell(key, part):
    offsets = jax.random.randint(key, (SLICES, OBS), 0, ROWS_DEV * COLS)
    slab_of = jnp.arange(OBS, dtype=jnp.int32) // OBS_DEV * (ROWS_DEV * COLS)
    cells = offsets.astype(jnp.int32) + slab_of[None, :]
    cells = cells.at[0, 0].set(0)
    cells = cells.at[SLICES - 1, OBS - 1].set(NY * COLS - 1)
    return cells.astype(jnp.int32)


def levels(rng, dims, pieces, low, top_value):
    def one(dim, shards_of):
        heights = jax.random.uniform(jax.random.fold_in(jax.random.fold_in(rng, 6), dim), (shards_of,), jnp.float32, low / len(pieces), top_value / len(pieces))
        return jnp.repeat(jnp.exp(heights), dims[dim] // shards_of).reshape((-1,) + (1,) * (len(dims) - dim - 1))

    loudness = one(*pieces[0])
    for cut in pieces[1:]:
        loudness = loudness * one(*cut)
    return loudness


def centred(key, shape, scale, most, pieces=(), held_as=jnp.bfloat16):
    gain = levels(key, shape, pieces, -0.22, 0.18) if pieces else 1.0
    drawn = jax.random.normal(key, shape, jnp.float32) * scale * gain
    return jnp.minimum(jnp.maximum(drawn, -most), most).astype(held_as)


def setup_inputs(seed: int = 0) -> dict:
    arg_keys = jax.random.split(jax.random.key(seed), 11)
    start_states = centred(arg_keys[0], (SLICES, MEMBERS, NY, COLS), 1.0, 6.0, ((0, 4), (1, 2), (2, 4)), jnp.float32)
    velocity_x = jnp.clip(jax.random.uniform(arg_keys[1], (NY, COLS), jnp.float32, -0.15, 0.15) * levels(arg_keys[1], (NY, COLS), ((0, 4),), -0.4, 0.0), -0.15, 0.15)
    velocity_y = jnp.clip(jax.random.uniform(arg_keys[2], (NY, COLS), jnp.float32, -0.15, 0.15) * levels(arg_keys[2], (NY, COLS), ((0, 4),), -0.4, 0.0), -0.15, 0.15)
    diffusivity = jnp.clip(jnp.exp(math.log(0.2) - 1.2039728 * jax.random.uniform(arg_keys[3], (NY, COLS), jnp.float32) ** levels(arg_keys[3], (NY, COLS), ((0, 4),), -0.2, 0.2)), 0.06, 0.2)
    source_shape = centred(arg_keys[4], (NY, COLS), 1.0, 6.0, ((0, 4),), jnp.float32)
    params = centred(arg_keys[5], (MEMBERS, PARAMS), 1.0, 6.0, ((0, 2),), jnp.float32)
    obs_cell = draw_obs_cell(jax.random.fold_in(arg_keys[10], 71), 0)
    obs_data = centred(arg_keys[7], (SLICES, OBS), 1.0, 6.0, ((0, 4), (1, 4)), jnp.float32)
    obs_noise = centred(arg_keys[8], (SLICES, OBS, MEMBERS), 0.5, 6.0, ((0, 4), (1, 4)), jnp.float32)
    obs_var = jnp.clip(jnp.exp(math.log(0.5) - 2.3025851 * jax.random.uniform(arg_keys[9], (SLICES, OBS), jnp.float32) ** levels(arg_keys[9], (SLICES, OBS), ((0, 4), (1, 4)), -0.2, 0.2)), 0.05, 0.5)
    return dict(start_states=start_states, velocity_x=velocity_x, velocity_y=velocity_y, diffusivity=diffusivity, source_shape=source_shape, params=params, obs_cell=obs_cell, obs_data=obs_data, obs_noise=obs_noise, obs_var=obs_var)


FINE_DT = 0.25

def advance(values_in, coeffs, inside, step_size, forcing):
    middle = values_in[:, 1:-1, :]
    above_row = values_in[:, :-2, :]
    below_row = values_in[:, 2:, :]
    west_cell = jnp.pad(middle[:, :, :-1], ((0, 0), (0, 0), (1, 0)))
    east_cell = jnp.pad(middle[:, :, 1:], ((0, 0), (0, 0), (0, 1)))
    spread_term = coeffs[0] * (above_row + below_row + west_cell + east_cell - 4.0 * middle)
    tendency = spread_term - coeffs[1] * (east_cell - west_cell) * 0.5 - coeffs[2] * (below_row - above_row) * 0.5
    if forcing is not None:
        tendency = tendency + forcing
    return (middle + step_size * tendency) * inside

def padded(values_in):
    return jnp.pad(values_in, ((0, 0), (1, 1), (0, 0)))

def reference(start_states, velocity_x, velocity_y, diffusivity, source_shape, params, obs_cell, obs_data, obs_noise, obs_var):
    coarse_dt = FINE_DT * FINE
    coeffs = jnp.stack([diffusivity, velocity_x, velocity_y])
    inside = jnp.ones((NY, 1), jnp.float32)
    forcing = source_shape[None] * jnp.repeat(params, BAND, axis=1)[:, None, :]
    results = []
    running = None
    for slice_no in range(SLICES):
        state = start_states[slice_no]
        current = state
        for section in range(FINE):
            current = advance(padded(current), coeffs, inside, FINE_DT, forcing)
        if slice_no == 0:
            running = current
        else:
            correction = current - advance(padded(state), coeffs, inside, coarse_dt, None)
            running = correction + advance(padded(running), coeffs, inside, coarse_dt, None)
        results.append(running)
    new_states = jnp.stack(results)
    flat = new_states.reshape(SLICES, MEMBERS, NY * COLS)
    where_obs = jnp.broadcast_to(obs_cell[:, None, :], (SLICES, MEMBERS, OBS))
    predicted = jnp.take_along_axis(flat, where_obs, axis=2)
    norm_factor = 1.0 / math.sqrt(MEMBERS - 1)
    inv_spread = lax.rsqrt(obs_var)[:, None, :]
    pred_mean = lax.optimization_barrier(jnp.mean(predicted, axis=1, keepdims=True))
    anomaly = (predicted - pred_mean) * (inv_spread * norm_factor)
    misfit = (obs_data[:, None, :] + jnp.transpose(obs_noise, (0, 2, 1)) - predicted) * inv_spread
    gram = jnp.einsum('sjo,sko->jk', anomaly, anomaly, precision=lax.Precision.HIGHEST)
    cross = jnp.einsum('sjo,sko->jk', anomaly, misfit, precision=lax.Precision.HIGHEST)
    system = jnp.eye(MEMBERS, dtype=jnp.float32) + gram
    factor = jnp.linalg.cholesky(system)
    weights = jax.scipy.linalg.cho_solve((factor, True), cross)
    param_anom = params - lax.optimization_barrier(jnp.mean(params, axis=0))
    new_params = params + jnp.dot(weights.T, param_anom, precision=lax.Precision.HIGHEST) * norm_factor
    return (new_states, new_params)
```

```python
import functools
import math

import jax
import jax.numpy as jnp
from jax import lax
from jax.experimental import pallas as pl
from jax.experimental.pallas import tpu as pltpu
from jax.sharding import PartitionSpec as P

FINE = 4
FINE_DT = 0.25
PAD = 8
MESH = pl.DeviceIdType.MESH
HIGH = lax.Precision.HIGHEST
NT = (((1,), (1,)), ((), ()))
TN = (((0,), (0,)), ((), ()))


def kernel(
    sizes,
    start_ref, vx_ref, vy_ref, diff_ref, src_ref, params_ref,
    cell_ref, data_ref, noise_ref, var_ref,
    out_ref, new_params_ref,
    st, a1, a2, a3, nw, rv, craw, cf, par, pall, xall, gtm, gsp,
    halo_send, halo_recv, row_send, row_recv, edge_send, edge_recv,
    ens_send, ens_recv, tm_send, tm_recv, sp_send, sp_recv,
):
    n_tm, n_sp, n_ens = sizes
    me_tm = lax.axis_index("tm")
    me_sp = lax.axis_index("space")
    me_ens = lax.axis_index("ens")
    members, rows, cols = start_ref.shape
    half = rows // 2
    bands = params_ref.shape[1]
    n_obs = data_ref.shape[1]
    other = 1 - me_ens
    first, last = me_sp == 0, me_sp == n_sp - 1
    up_sp = lax.rem(me_sp + n_sp - 1, n_sp)
    dn_sp = lax.rem(me_sp + 1, n_sp)
    next_tm = lax.rem(me_tm + 1, n_tm)
    prev_tm = lax.rem(me_tm + n_tm - 1, n_tm)

    barrier = pltpu.get_barrier_semaphore()
    greeted = [{"ens": other}]
    greeted += [{"tm": lax.rem(me_tm + k, n_tm)} for k in range(1, n_tm)]
    greeted += [{"space": lax.rem(me_sp + k, n_sp)} for k in range(1, n_sp)]
    greeted += [{"tm": t, "space": s} for t in (next_tm, prev_tm) for s in (up_sp, dn_sp)]
    for device in greeted:
        pl.semaphore_signal(barrier, inc=1, device_id=device, device_id_type=MESH)

    for k, ref in enumerate((diff_ref, vx_ref, vy_ref, src_ref)):
        craw[k, PAD:PAD + rows, :] = ref[...]

    @pl.loop(0, rows // 8)
    def _(k):
        at = pl.multiple_of(k * 8, 8)
        st[pl.ds(PAD + at, 8)] = jnp.swapaxes(start_ref[:, pl.ds(at, 8), :], 0, 1)

    pl.semaphore_wait(barrier, len(greeted))

    def remote(src, dst, send, recv, device):
        return pltpu.make_async_remote_copy(
            src_ref=src, dst_ref=dst, send_sem=send, recv_sem=recv,
            device_id=device, device_id_type=MESH,
        )

    up = {"space": up_sp}
    down = {"space": dn_sp}
    coef_up = remote(craw.at[:, pl.ds(PAD, 8)], craw.at[:, pl.ds(PAD + rows, 8)],
                     halo_send.at[0], halo_recv.at[0], up)
    coef_down = remote(craw.at[:, pl.ds(PAD + rows - 8, 8)], craw.at[:, pl.ds(0, 8)],
                       halo_send.at[1], halo_recv.at[1], down)
    state_up = remote(st.at[pl.ds(PAD, FINE)], st.at[pl.ds(PAD + rows, FINE)],
                      halo_send.at[2], halo_recv.at[2], up)
    state_down = remote(st.at[pl.ds(PAD + rows - FINE, FINE)], st.at[pl.ds(PAD - FINE, FINE)],
                        halo_send.at[3], halo_recv.at[3], down)

    @pl.when(jnp.logical_not(first))
    def _():
        coef_up.start()
        state_up.start()

    @pl.when(jnp.logical_not(last))
    def _():
        coef_down.start()
        state_down.start()

    share_params = remote(params_ref, pall.at[me_ens], ens_send.at[0], ens_recv.at[0], {"ens": other})
    share_params.start()
    pall[me_ens] = params_ref[...]

    @pl.when(first)
    def _():
        craw[:, 0:PAD, :] = jnp.zeros((4, PAD, cols), jnp.float32)
        st[0:PAD] = jnp.zeros((PAD, members, cols), jnp.float32)
        rv[0] = jnp.zeros((members, cols), jnp.float32)

    @pl.when(last)
    def _():
        craw[:, PAD + rows:, :] = jnp.zeros((4, PAD, cols), jnp.float32)
        st[PAD + rows:] = jnp.zeros((PAD, members, cols), jnp.float32)
        rv[rows + 1] = jnp.zeros((members, cols), jnp.float32)

    pick = (lax.broadcasted_iota(jnp.int32, (bands, cols), 1) // (cols // bands)
            == lax.broadcasted_iota(jnp.int32, (bands, cols), 0)).astype(jnp.float32)
    par[...] = jnp.dot(params_ref[...], pick, precision=HIGH, preferred_element_type=jnp.float32)

    mine = (lax.broadcasted_iota(jnp.int32, (members, members * n_ens), 1)
            == lax.broadcasted_iota(jnp.int32, (members, members * n_ens), 0) + me_ens * members)
    noise = lax.dot_general(mine.astype(jnp.float32), noise_ref[0], NT, precision=HIGH,
                            preferred_element_type=jnp.float32)
    target = data_ref[...] + noise
    inv_spread = lax.rsqrt(var_ref[...])

    @pl.when(jnp.logical_not(last))
    def _():
        coef_up.wait_recv()
        state_up.wait_recv()

    @pl.when(jnp.logical_not(first))
    def _():
        coef_down.wait_recv()
        state_down.wait_recv()

    lane = lax.broadcasted_iota(jnp.int32, (8, cols), 1)

    @pl.loop(0, (rows + 2 * PAD) // 8)
    def _(k):
        at = pl.ds(pl.multiple_of(k * 8, 8), 8)
        d = craw[0, at, :] * FINE_DT
        hx = craw[1, at, :] * (0.5 * FINE_DT)
        hy = craw[2, at, :] * (0.5 * FINE_DT)
        parts = [
            -4.0 * d, d + hy, d - hy,
            jnp.where(lane == 0, 0.0, d + hx),
            jnp.where(lane == cols - 1, 0.0, d - hx),
            craw[3, at, :] * FINE_DT, d, d,
        ]
        cf[at] = jnp.swapaxes(jnp.stack(parts, axis=0), 0, 1)

    def spread(row, above, middle, below):
        c = [cf[row + PAD, k:k + 1, :] for k in range(5)]
        return (c[0] * middle + c[1] * above + c[2] * below
                + c[3] * pltpu.roll(middle, 1, 1) + c[4] * pltpu.roll(middle, cols - 1, 1))

    def fine(field, row):
        at = row + PAD
        middle = field[at]
        force = cf[at, 5:6, :] * par[...]
        return middle + (spread(row, field[at - 1], middle, field[at + 1]) + force)

    def row_copy(row):
        return remote(nw.at[row], rv.at[row + 1], row_send.at[row], row_recv.at[row], {"tm": next_tm})

    edge_up = remote(nw.at[0], rv.at[rows + 1], edge_send.at[0], edge_recv.at[0],
                     {"tm": next_tm, "space": up_sp})
    edge_down = remote(nw.at[rows - 1], rv.at[0], edge_send.at[1], edge_recv.at[1],
                       {"tm": next_tm, "space": dn_sp})
    sends = me_tm < n_tm - 1
    receives = me_tm > 0

    def coarse(row):
        above, middle, below = (rv[row + k] - st[row + PAD - 1 + k] for k in range(3))
        return middle + spread(row, above, middle, below) * float(FINE)

    @pl.loop(0, half + 6)
    def _(step):
        t = step - 3
        for top in (True, False):
            def place(r):
                return r if top else rows - 1 - r
            a1[place(t) + PAD] = fine(st, place(t))
            a2[place(t - 1) + PAD] = fine(a1, place(t - 1))
            a3[place(t - 2) + PAD] = fine(a2, place(t - 2))
        q = t - 3

        @pl.when(q >= 0)
        def _():
            nw[q] = fine(a3, q)
            nw[rows - 1 - q] = fine(a3, rows - 1 - q)

            @pl.when(receives)
            def _():
                @pl.when(q == 0)
                def _():
                    row_copy(0).wait_recv()
                    row_copy(rows - 1).wait_recv()

                    @pl.when(jnp.logical_not(last))
                    def _():
                        edge_up.wait_recv()

                    @pl.when(jnp.logical_not(first))
                    def _():
                        edge_down.wait_recv()

                @pl.when(q < half - 1)
                def _():
                    row_copy(q + 1).wait_recv()
                    row_copy(rows - 2 - q).wait_recv()

                nw[q] = nw[q] + coarse(q)
                nw[rows - 1 - q] = nw[rows - 1 - q] + coarse(rows - 1 - q)

            @pl.when(sends)
            def _():
                @pl.when(q == 0)
                def _():
                    @pl.when(jnp.logical_not(first))
                    def _():
                        edge_up.start()

                    @pl.when(jnp.logical_not(last))
                    def _():
                        edge_down.start()

                row_copy(q).start()
                row_copy(rows - 1 - q).start()

    lanes = lax.broadcasted_iota(jnp.int32, (members, 128), 1)
    wide = lax.broadcasted_iota(jnp.int32, (members, cols), 1)

    def gather(o, found):
        cell = lax.rem(cell_ref[0, o], rows * cols)
        row = lax.div(cell, cols)
        col = lax.rem(cell, cols)
        value = jnp.sum(jnp.where(wide == col, nw[row], 0.0), axis=1, keepdims=True)
        return jnp.where(lanes == o, value, found)

    found = lax.fori_loop(0, n_obs, gather, jnp.zeros((members, 128), jnp.float32), unroll=8)
    predicted = found[:, :n_obs]
    xall[me_ens] = jnp.concatenate(
        [predicted * inv_spread, (target - predicted) * inv_spread], axis=1)
    share_pred = remote(xall.at[me_ens], xall.at[me_ens], ens_send.at[1], ens_recv.at[1], {"ens": other})
    share_pred.start()

    @pl.loop(0, rows // 8)
    def _(k):
        at = pl.multiple_of(k * 8, 8)
        out_ref[:, pl.ds(at, 8), :] = jnp.swapaxes(nw[pl.ds(at, 8)], 0, 1)

    share_pred.wait()
    total = members * n_ens
    norm_factor = 1.0 / math.sqrt(total - 1)
    everyone = jnp.concatenate([xall[e] for e in range(n_ens)], axis=0)
    scaled, misfit = everyone[:, :n_obs], everyone[:, n_obs:]
    anomaly = (scaled - jnp.mean(scaled, axis=0, keepdims=True)) * norm_factor
    right = jnp.concatenate(
        [anomaly, misfit, jnp.zeros((128 - 2 * total, n_obs), jnp.float32)], axis=0)
    gtm[me_tm] = lax.dot_general(anomaly, right, NT, precision=HIGH,
                                 preferred_element_type=jnp.float32)

    def add_up(buffer, axis, me, count, send, recv):
        peers = [lax.rem(me + k, count) for k in range(1, count)]
        for peer in peers:
            remote(buffer.at[me], buffer.at[me], send.at[peer], recv.at[me], {axis: peer}).start()
        for peer in peers:
            remote(buffer.at[peer], buffer.at[peer], send.at[peer], recv.at[peer], {axis: peer}).wait_recv()
        summed = buffer[0]
        for k in range(1, count):
            summed = summed + buffer[k]
        return summed, peers

    summed, tm_peers = add_up(gtm, "tm", me_tm, n_tm, tm_send, tm_recv)
    gsp[me_sp] = summed
    system, sp_peers = add_up(gsp, "space", me_sp, n_sp, sp_send, sp_recv)

    row_no = lax.broadcasted_iota(jnp.int32, (total, 128), 0)
    system = system + (row_no == lax.broadcasted_iota(jnp.int32, (total, 128), 1)).astype(jnp.float32)
    for k in range(total):
        pivot_row = system[k:k + 1, :] / system[k:k + 1, k:k + 1]
        system = jnp.where(row_no == k, pivot_row, system - system[:, k:k + 1] * pivot_row)
    weights = system[:, total:2 * total]

    share_params.wait()
    every_param = jnp.concatenate([pall[e] for e in range(n_ens)], axis=0)
    param_anom = every_param - jnp.mean(every_param, axis=0, keepdims=True)
    update = lax.dot_general(weights, param_anom, TN, precision=HIGH,
                             preferred_element_type=jnp.float32) * norm_factor
    own = jnp.where(me_ens == 0, update[:members], update[members:])
    new_params_ref[...] = params_ref[...] + own

    @pl.when(jnp.logical_not(first))
    def _():
        coef_up.wait_send()
        state_up.wait_send()

    @pl.when(jnp.logical_not(last))
    def _():
        coef_down.wait_send()
        state_down.wait_send()

    @pl.when(sends)
    def _():
        @pl.when(jnp.logical_not(first))
        def _():
            edge_up.wait_send()

        @pl.when(jnp.logical_not(last))
        def _():
            edge_down.wait_send()

        @pl.loop(0, rows)
        def _(row):
            row_copy(row).wait_send()

    for peer in tm_peers:
        remote(gtm.at[me_tm], gtm.at[me_tm], tm_send.at[peer], tm_recv.at[me_tm], {"tm": peer}).wait_send()
    for peer in sp_peers:
        remote(gsp.at[me_sp], gsp.at[me_sp], sp_send.at[peer], sp_recv.at[me_sp], {"space": peer}).wait_send()


def per_device(sizes, start_states, velocity_x, velocity_y, diffusivity, source_shape, params,
               obs_cell, obs_data, obs_noise, obs_var):
    state = start_states[0]
    members, rows, cols = state.shape
    n_tm, n_sp, n_ens = sizes
    total = members * n_ens
    padded = (rows + 2 * PAD, members, cols)
    f32 = jnp.float32
    vmem = pl.BlockSpec(memory_space=pltpu.VMEM)
    dma = pltpu.SemaphoreType.DMA
    new_states, new_params = pl.pallas_call(
        functools.partial(kernel, sizes),
        out_shape=(jax.ShapeDtypeStruct(state.shape, f32), jax.ShapeDtypeStruct(params.shape, f32)),
        in_specs=[vmem] * 6 + [pl.BlockSpec(memory_space=pltpu.SMEM)] + [vmem] * 3,
        out_specs=(vmem, vmem),
        scratch_shapes=[
            pltpu.VMEM(padded, f32),
            pltpu.VMEM(padded, f32),
            pltpu.VMEM(padded, f32),
            pltpu.VMEM(padded, f32),
            pltpu.VMEM((rows, members, cols), f32),
            pltpu.VMEM((rows + 2, members, cols), f32),
            pltpu.VMEM((4, rows + 2 * PAD, cols), f32),
            pltpu.VMEM((rows + 2 * PAD, 8, cols), f32),
            pltpu.VMEM((members, cols), f32),
            pltpu.VMEM((n_ens,) + params.shape, f32),
            pltpu.VMEM((n_ens, members, 128), f32),
            pltpu.VMEM((n_tm, total, 128), f32),
            pltpu.VMEM((n_sp, total, 128), f32),
            dma((4,)), dma((4,)),
            dma((rows,)), dma((rows,)),
            dma((2,)), dma((2,)),
            dma((2,)), dma((2,)),
            dma((n_tm,)), dma((n_tm,)),
            dma((n_sp,)), dma((n_sp,)),
        ],
        compiler_params=pltpu.CompilerParams(
            collective_id=0, has_side_effects=True, vmem_limit_bytes=48 * 2**20
        ),
    )(state, velocity_x, velocity_y, diffusivity, source_shape, params,
      obs_cell, obs_data, obs_noise, obs_var)
    return (new_states[None], new_params)


def solution(mesh):
    sizes = tuple(mesh.shape[axis] for axis in ("tm", "space", "ens"))
    in_specs = (
        P("tm", "ens", "space", None),
        P("space", None),
        P("space", None),
        P("space", None),
        P("space", None),
        P("ens", None),
        P("tm", "space"),
        P("tm", "space"),
        P("tm", "space", None),
        P("tm", "space"),
    )
    out_specs = (P("tm", "ens", "space", None), P("ens", None))
    return jax.shard_map(
        functools.partial(per_device, sizes), mesh=mesh,
        in_specs=in_specs, out_specs=out_specs, check_vma=False,
    )
```

```python
import functools
import math

import jax
import jax.numpy as jnp
from jax import lax
from jax.experimental import pallas as pl
from jax.experimental.pallas import tpu as pltpu
from jax.sharding import PartitionSpec as P

FINE = 4
FINE_DT = 0.25
PAD = 8
MESH = pl.DeviceIdType.MESH
HIGH = lax.Precision.HIGHEST
NT = (((1,), (1,)), ((), ()))
TN = (((0,), (0,)), ((), ()))


def kernel(
    sizes,
    start_hbm, vx_hbm, vy_hbm, diff_hbm, src_hbm, params_hbm,
    cell_hbm, data_hbm, noise_hbm, var_hbm,
    out_hbm, new_params_ref,
    start_ref, out_ref, params_ref, cell_ref, data_ref, noise_ref, var_ref,
    st, a1, a2, a3, nw, rv, craw, cf, par, pall, xall, gtm, gsp,
    in_sem, small_sem, block_sem, out_sem,
    halo_send, halo_recv, row_send, row_recv, edge_send, edge_recv,
    ens_send, ens_recv, tm_send, tm_recv, sp_send, sp_recv,
):
    n_tm, n_sp, n_ens = sizes
    me_tm = lax.axis_index("tm")
    me_sp = lax.axis_index("space")
    me_ens = lax.axis_index("ens")
    members, rows, cols = start_ref.shape
    half = rows // 2
    pairs = half // 8
    bands = params_ref.shape[1]
    n_obs = data_ref.shape[1]
    other = 1 - me_ens
    first, last = me_sp == 0, me_sp == n_sp - 1
    up_sp = lax.rem(me_sp + n_sp - 1, n_sp)
    dn_sp = lax.rem(me_sp + 1, n_sp)
    next_tm = lax.rem(me_tm + 1, n_tm)
    prev_tm = lax.rem(me_tm + n_tm - 1, n_tm)
    sends = me_tm < n_tm - 1
    receives = me_tm > 0

    def block_of(pair, side):
        at = half - 8 - 8 * pair if side == 0 else half + 8 * pair
        return at if isinstance(pair, int) else pl.multiple_of(at, 8)

    def start_in(pair, side):
        at = pl.ds(block_of(pair, side), 8)
        return pltpu.make_async_copy(start_hbm.at[:, at], start_ref.at[:, at], block_sem.at[side, pair])

    def coef_in(k):
        ref = (diff_hbm, vx_hbm, vy_hbm, src_hbm)[k]
        return pltpu.make_async_copy(ref, craw.at[k, pl.ds(PAD, rows)], in_sem.at[k])

    def result_out(pair, side):
        at = pl.ds(block_of(pair, side), 8)
        return pltpu.make_async_copy(out_ref.at[:, at], out_hbm.at[:, at], out_sem.at[side, pair])

    small = [
        pltpu.make_async_copy(src, dst, small_sem.at[k])
        for k, (src, dst) in enumerate((
            (params_hbm, params_ref), (cell_hbm, cell_ref), (data_hbm, data_ref),
            (noise_hbm, noise_ref), (var_hbm, var_ref)))
    ]
    start_in(0, 0).start()
    start_in(0, 1).start()
    for k in range(4):
        coef_in(k).start()
    for copy in small:
        copy.start()
    for pair in range(1, pairs):
        start_in(pair, 0).start()
        start_in(pair, 1).start()

    barrier = pltpu.get_barrier_semaphore()
    greeted = [{"ens": other}]
    greeted += [{"tm": lax.rem(me_tm + k, n_tm)} for k in range(1, n_tm)]
    greeted += [{"space": lax.rem(me_sp + k, n_sp)} for k in range(1, n_sp)]
    greeted += [{"tm": t, "space": s} for t in (next_tm, prev_tm) for s in (up_sp, dn_sp)]
    for device in greeted:
        pl.semaphore_signal(barrier, inc=1, device_id=device, device_id_type=MESH)

    def remote(src, dst, send, recv, device):
        return pltpu.make_async_remote_copy(
            src_ref=src, dst_ref=dst, send_sem=send, recv_sem=recv,
            device_id=device, device_id_type=MESH,
        )

    up = {"space": up_sp}
    down = {"space": dn_sp}
    coef_up = remote(craw.at[:, pl.ds(PAD, 8)], craw.at[:, pl.ds(PAD + rows, 8)],
                     halo_send.at[0], halo_recv.at[0], up)
    coef_down = remote(craw.at[:, pl.ds(PAD + rows - 8, 8)], craw.at[:, pl.ds(0, 8)],
                       halo_send.at[1], halo_recv.at[1], down)
    state_up = remote(st.at[pl.ds(PAD, FINE)], st.at[pl.ds(PAD + rows, FINE)],
                      halo_send.at[2], halo_recv.at[2], up)
    state_down = remote(st.at[pl.ds(PAD + rows - FINE, FINE)], st.at[pl.ds(PAD - FINE, FINE)],
                        halo_send.at[3], halo_recv.at[3], down)

    lane = lax.broadcasted_iota(jnp.int32, (8, cols), 1)

    def build(at):
        at = pl.ds(at, 8)
        d = craw[0, at, :] * FINE_DT
        hx = craw[1, at, :] * (0.5 * FINE_DT)
        hy = craw[2, at, :] * (0.5 * FINE_DT)
        parts = [
            -4.0 * d, d + hy, d - hy,
            jnp.where(lane == 0, 0.0, d + hx),
            jnp.where(lane == cols - 1, 0.0, d - hx),
            craw[3, at, :] * FINE_DT, d, d,
        ]
        cf[at] = jnp.swapaxes(jnp.stack(parts, axis=0), 0, 1)

    def prepare(pair):
        for side in (0, 1):
            start_in(pair, side).wait()
            at = block_of(pair, side)
            st[pl.ds(PAD + at, 8)] = jnp.swapaxes(start_ref[:, pl.ds(at, 8), :], 0, 1)
            build(PAD + at if isinstance(pair, int) else pl.multiple_of(PAD + at, 8))

    small[0].wait()
    pick = (lax.broadcasted_iota(jnp.int32, (bands, cols), 1) // (cols // bands)
            == lax.broadcasted_iota(jnp.int32, (bands, cols), 0)).astype(jnp.float32)
    par[...] = jnp.dot(params_ref[...], pick, precision=HIGH, preferred_element_type=jnp.float32)
    pall[me_ens] = params_ref[...]
    for k in range(4):
        coef_in(k).wait()
    prepare(0)

    @pl.when(first)
    def _():
        craw[:, 0:PAD, :] = jnp.zeros((4, PAD, cols), jnp.float32)
        st[0:PAD] = jnp.zeros((PAD, members, cols), jnp.float32)
        rv[0] = jnp.zeros((members, cols), jnp.float32)

    @pl.when(last)
    def _():
        craw[:, PAD + rows:, :] = jnp.zeros((4, PAD, cols), jnp.float32)
        st[PAD + rows:] = jnp.zeros((PAD, members, cols), jnp.float32)
        rv[rows + 1] = jnp.zeros((members, cols), jnp.float32)

    pl.semaphore_wait(barrier, len(greeted))
    share_params = remote(params_ref, pall.at[me_ens], ens_send.at[0], ens_recv.at[0], {"ens": other})
    share_params.start()

    @pl.when(jnp.logical_not(first))
    def _():
        coef_up.start()

    @pl.when(jnp.logical_not(last))
    def _():
        coef_down.start()

    def spread(row, above, middle, below):
        c = [cf[row + PAD, k:k + 1, :] for k in range(5)]
        return (c[0] * middle + c[1] * above + c[2] * below
                + c[3] * pltpu.roll(middle, 1, 1) + c[4] * pltpu.roll(middle, cols - 1, 1))

    def fine(field, row):
        at = row + PAD
        middle = field[at]
        force = cf[at, 5:6, :] * par[...]
        return middle + (spread(row, field[at - 1], middle, field[at + 1]) + force)

    def coarse(row):
        above, middle, below = (rv[row + k] - st[row + PAD - 1 + k] for k in range(3))
        return middle + spread(row, above, middle, below) * float(FINE)

    def row_copy(row):
        return remote(nw.at[row], rv.at[row + 1], row_send.at[row], row_recv.at[row], {"tm": next_tm})

    edge_up = remote(nw.at[0], rv.at[rows + 1], edge_send.at[0], edge_recv.at[0],
                     {"tm": next_tm, "space": up_sp})
    edge_down = remote(nw.at[rows - 1], rv.at[0], edge_send.at[1], edge_recv.at[1],
                       {"tm": next_tm, "space": dn_sp})

    def both(away):
        return half - 1 - away, half + away

    def finish(pair):
        for side in (0, 1):
            at = block_of(pair, side)
            out_ref[:, pl.ds(at, 8), :] = jnp.swapaxes(nw[pl.ds(at, 8)], 0, 1)
            result_out(pair, side).start()

    def fine_both(field, away):
        return [fine(field, row) for row in both(away)]

    def keep(field, away, values):
        for row, value in zip(both(away), values):
            field[row + PAD] = value

    @pl.loop(0, half + 3)
    def _(t):
        keep(a1, t, fine_both(st, t))
        keep(a2, t - 1, fine_both(a1, t - 1))
        keep(a3, t - 2, fine_both(a2, t - 2))
        q = t - 3

        @pl.when(q >= 0)
        def _():
            upper, lower = both(q)
            values = fine_both(a3, q)
            nw[upper] = values[0]
            nw[lower] = values[1]

            @pl.when(receives)
            def _():
                @pl.when(q == 0)
                def _():
                    row_copy(half - 1).wait_recv()
                    row_copy(half).wait_recv()

                @pl.when(q < half - 1)
                def _():
                    row_copy(upper - 1).wait_recv()
                    row_copy(lower + 1).wait_recv()

                @pl.when(q == half - 1)
                def _():
                    @pl.when(jnp.logical_not(last))
                    def _():
                        edge_up.wait_recv()

                    @pl.when(jnp.logical_not(first))
                    def _():
                        edge_down.wait_recv()

                more = [coarse(upper), coarse(lower)]
                nw[upper] = nw[upper] + more[0]
                nw[lower] = nw[lower] + more[1]

            @pl.when(sends)
            def _():
                @pl.when(q == half - 1)
                def _():
                    @pl.when(jnp.logical_not(first))
                    def _():
                        edge_up.start()

                    @pl.when(jnp.logical_not(last))
                    def _():
                        edge_down.start()

                row_copy(upper).start()
                row_copy(lower).start()

            @pl.when(jnp.logical_and(lax.rem(q, 8) == 7, q < half - 1))
            def _():
                finish(q // 8)

        @pl.when(jnp.logical_and(lax.rem(t, 8) == 6, t < half - 2))
        def _():
            prepare((t + 2) // 8)

        @pl.when(t == half - 9)
        def _():
            @pl.when(jnp.logical_not(first))
            def _():
                state_up.start()

            @pl.when(jnp.logical_not(last))
            def _():
                state_down.start()

        @pl.when(t == half - 2)
        def _():
            @pl.when(jnp.logical_not(last))
            def _():
                coef_up.wait_recv()
                state_up.wait_recv()

            @pl.when(jnp.logical_not(first))
            def _():
                coef_down.wait_recv()
                state_down.wait_recv()

            build(0)
            build(PAD + rows)

    for copy in small[1:]:
        copy.wait()
    mine = (lax.broadcasted_iota(jnp.int32, (members, members * n_ens), 1)
            == lax.broadcasted_iota(jnp.int32, (members, members * n_ens), 0) + me_ens * members)
    noise = lax.dot_general(mine.astype(jnp.float32), noise_ref[...], (((1,), (0,)), ((), ())),
                            precision=HIGH, preferred_element_type=jnp.float32)
    target = data_ref[...] + noise
    inv_spread = lax.rsqrt(var_ref[...])

    lanes = lax.broadcasted_iota(jnp.int32, (members, 128), 1)
    wide = lax.broadcasted_iota(jnp.int32, (members, cols), 1)

    def gather(o, found):
        cell = lax.rem(cell_ref[0, o], rows * cols)
        row = lax.div(cell, cols)
        col = lax.rem(cell, cols)
        value = jnp.sum(jnp.where(wide == col, nw[row], 0.0), axis=1, keepdims=True)
        return jnp.where(lanes == o, value, found)

    found = lax.fori_loop(0, n_obs, gather, jnp.zeros((members, 128), jnp.float32), unroll=8)
    predicted = found[:, :n_obs]
    xall[me_ens] = jnp.concatenate(
        [predicted * inv_spread, (target - predicted) * inv_spread], axis=1)
    share_pred = remote(xall.at[me_ens], xall.at[me_ens], ens_send.at[1], ens_recv.at[1], {"ens": other})
    share_pred.start()

    finish(pairs - 1)
    share_pred.wait()
    total = members * n_ens
    norm_factor = 1.0 / math.sqrt(total - 1)
    everyone = jnp.concatenate([xall[e] for e in range(n_ens)], axis=0)
    scaled, misfit = everyone[:, :n_obs], everyone[:, n_obs:]
    anomaly = (scaled - jnp.mean(scaled, axis=0, keepdims=True)) * norm_factor
    right = jnp.concatenate(
        [anomaly, misfit, jnp.zeros((128 - 2 * total, n_obs), jnp.float32)], axis=0)
    gtm[me_tm] = lax.dot_general(anomaly, right, NT, precision=HIGH,
                                 preferred_element_type=jnp.float32)

    def add_up(buffer, axis, me, count, send, recv):
        peers = [lax.rem(me + k, count) for k in range(1, count)]
        for peer in peers:
            remote(buffer.at[me], buffer.at[me], send.at[peer], recv.at[me], {axis: peer}).start()
        for peer in peers:
            remote(buffer.at[peer], buffer.at[peer], send.at[peer], recv.at[peer], {axis: peer}).wait_recv()
        summed = buffer[0]
        for k in range(1, count):
            summed = summed + buffer[k]
        return summed, peers

    summed, tm_peers = add_up(gtm, "tm", me_tm, n_tm, tm_send, tm_recv)
    gsp[me_sp] = summed
    system, sp_peers = add_up(gsp, "space", me_sp, n_sp, sp_send, sp_recv)

    row_no = lax.broadcasted_iota(jnp.int32, (total, 128), 0)
    system = system + (row_no == lax.broadcasted_iota(jnp.int32, (total, 128), 1)).astype(jnp.float32)
    for k in range(total):
        pivot_row = system[k:k + 1, :] / system[k:k + 1, k:k + 1]
        system = jnp.where(row_no == k, pivot_row, system - system[:, k:k + 1] * pivot_row)
    weights = system[:, total:2 * total]

    share_params.wait()
    every_param = jnp.concatenate([pall[e] for e in range(n_ens)], axis=0)
    param_anom = every_param - jnp.mean(every_param, axis=0, keepdims=True)
    update = lax.dot_general(weights, param_anom, TN, precision=HIGH,
                             preferred_element_type=jnp.float32) * norm_factor
    own = jnp.where(me_ens == 0, update[:members], update[members:])
    new_params_ref[...] = params_ref[...] + own

    for pair in range(pairs):
        for side in (0, 1):
            result_out(pair, side).wait()

    @pl.when(jnp.logical_not(first))
    def _():
        coef_up.wait_send()
        state_up.wait_send()

    @pl.when(jnp.logical_not(last))
    def _():
        coef_down.wait_send()
        state_down.wait_send()

    @pl.when(sends)
    def _():
        @pl.when(jnp.logical_not(first))
        def _():
            edge_up.wait_send()

        @pl.when(jnp.logical_not(last))
        def _():
            edge_down.wait_send()

        @pl.loop(0, rows)
        def _(row):
            row_copy(row).wait_send()

    for peer in tm_peers:
        remote(gtm.at[me_tm], gtm.at[me_tm], tm_send.at[peer], tm_recv.at[me_tm], {"tm": peer}).wait_send()
    for peer in sp_peers:
        remote(gsp.at[me_sp], gsp.at[me_sp], sp_send.at[peer], sp_recv.at[me_sp], {"space": peer}).wait_send()


def per_device(sizes, start_states, velocity_x, velocity_y, diffusivity, source_shape, params,
               obs_cell, obs_data, obs_noise, obs_var):
    state = start_states[0]
    members, rows, cols = state.shape
    n_tm, n_sp, n_ens = sizes
    total = members * n_ens
    padded = (rows + 2 * PAD, members, cols)
    f32 = jnp.float32
    vmem = pl.BlockSpec(memory_space=pltpu.VMEM)
    hbm = pl.BlockSpec(memory_space=pl.ANY)
    dma = pltpu.SemaphoreType.DMA
    pairs = rows // 16
    new_states, new_params = pl.pallas_call(
        functools.partial(kernel, sizes),
        out_shape=(jax.ShapeDtypeStruct(state.shape, f32), jax.ShapeDtypeStruct(params.shape, f32)),
        in_specs=[hbm] * 10,
        out_specs=(hbm, vmem),
        scratch_shapes=[
            pltpu.VMEM(state.shape, f32),
            pltpu.VMEM(state.shape, f32),
            pltpu.VMEM(params.shape, f32),
            pltpu.SMEM(obs_cell.shape, jnp.int32),
            pltpu.VMEM(obs_data.shape, f32),
            pltpu.VMEM((total, obs_data.shape[1]), f32),
            pltpu.VMEM(obs_var.shape, f32),
            pltpu.VMEM(padded, f32),
            pltpu.VMEM(padded, f32),
            pltpu.VMEM(padded, f32),
            pltpu.VMEM(padded, f32),
            pltpu.VMEM((rows, members, cols), f32),
            pltpu.VMEM((rows + 2, members, cols), f32),
            pltpu.VMEM((4, rows + 2 * PAD, cols), f32),
            pltpu.VMEM((rows + 2 * PAD, 8, cols), f32),
            pltpu.VMEM((members, cols), f32),
            pltpu.VMEM((n_ens,) + params.shape, f32),
            pltpu.VMEM((n_ens, members, 128), f32),
            pltpu.VMEM((n_tm, total, 128), f32),
            pltpu.VMEM((n_sp, total, 128), f32),
            dma((4,)), dma((5,)), dma((2, pairs)), dma((2, pairs)),
            dma((4,)), dma((4,)),
            dma((rows,)), dma((rows,)),
            dma((2,)), dma((2,)),
            dma((2,)), dma((2,)),
            dma((n_tm,)), dma((n_tm,)),
            dma((n_sp,)), dma((n_sp,)),
        ],
        compiler_params=pltpu.CompilerParams(
            collective_id=0, has_side_effects=True, vmem_limit_bytes=60 * 2**20
        ),
    )(state, velocity_x, velocity_y, diffusivity, source_shape, params,
      obs_cell, obs_data, jnp.swapaxes(obs_noise[0], 0, 1), obs_var)
    return (new_states[None], new_params)


def solution(mesh):
    sizes = tuple(mesh.shape[axis] for axis in ("tm", "space", "ens"))
    in_specs = (
        P("tm", "ens", "space", None),
        P("space", None),
        P("space", None),
        P("space", None),
        P("space", None),
        P("ens", None),
        P("tm", "space"),
        P("tm", "space"),
        P("tm", "space", None),
        P("tm", "space"),
    )
    out_specs = (P("tm", "ens", "space", None), P("ens", None))
    return jax.shard_map(
        functools.partial(per_device, sizes), mesh=mesh,
        in_specs=in_specs, out_specs=out_specs, check_vma=False,
    )
```

```python
import functools
import math

import jax
import jax.numpy as jnp
from jax import lax
from jax.experimental import pallas as pl
from jax.experimental.pallas import tpu as pltpu
from jax.sharding import PartitionSpec as P

FINE = 4
FINE_DT = 0.25
PAD = 8
AHEAD = 3
MESH = pl.DeviceIdType.MESH
HIGH = lax.Precision.HIGHEST
NT = (((1,), (1,)), ((), ()))
TN = (((0,), (0,)), ((), ()))


def kernel(
    sizes,
    start_hbm, vx_hbm, vy_hbm, diff_hbm, src_hbm, params_hbm,
    cell_hbm, data_hbm, noise_hbm, var_hbm,
    out_ref, new_params_ref,
    start_ref, params_ref, cell_ref, data_ref, noise_ref, var_ref,
    st, a1, a2, a3, nw, rv, craw, cf, par, pall, xall, sums,
    in_sem, small_sem, block_sem,
    halo_send, halo_recv, row_send, row_recv, edge_send, edge_recv,
    ens_send, ens_recv, sum_send, sum_recv,
):
    n_tm, n_sp, n_ens = sizes
    me_tm = lax.axis_index("tm")
    me_sp = lax.axis_index("space")
    me_ens = lax.axis_index("ens")
    members, rows, cols = start_ref.shape
    half = rows // 2
    pairs = half // 8
    bands = params_ref.shape[1]
    n_obs = data_ref.shape[1]
    other = 1 - me_ens
    first, last = me_sp == 0, me_sp == n_sp - 1
    up_sp = lax.rem(me_sp + n_sp - 1, n_sp)
    dn_sp = lax.rem(me_sp + 1, n_sp)
    next_tm = lax.rem(me_tm + 1, n_tm)
    sends = me_tm < n_tm - 1
    receives = me_tm > 0

    def block_of(pair, side):
        at = half - 8 - 8 * pair if side == 0 else half + 8 * pair
        return at if isinstance(pair, int) else pl.multiple_of(at, 8)

    def start_in(pair, side):
        at = pl.ds(block_of(pair, side), 8)
        return pltpu.make_async_copy(start_hbm.at[:, at], start_ref.at[:, at], block_sem.at[side, pair])

    def coef_in(k):
        ref = (diff_hbm, vx_hbm, vy_hbm, src_hbm)[k]
        return pltpu.make_async_copy(ref, craw.at[k, pl.ds(PAD, rows)], in_sem.at[k])

    small = [
        pltpu.make_async_copy(src, dst, small_sem.at[k])
        for k, (src, dst) in enumerate((
            (params_hbm, params_ref), (cell_hbm, cell_ref), (data_hbm, data_ref),
            (noise_hbm, noise_ref), (var_hbm, var_ref)))
    ]
    start_in(0, 0).start()
    start_in(0, 1).start()
    for k in range(4):
        coef_in(k).start()
    for copy in small:
        copy.start()
    for pair in range(1, pairs):
        start_in(pair, 0).start()
        start_in(pair, 1).start()

    barrier = pltpu.get_barrier_semaphore()
    chips = [(lax.rem(me_tm + t, n_tm), lax.rem(me_sp + z, n_sp))
             for t in range(n_tm) for z in range(n_sp) if t or z]
    greeted = [{"ens": other}] + [{"tm": t, "space": z} for t, z in chips]
    for device in greeted:
        pl.semaphore_signal(barrier, inc=1, device_id=device, device_id_type=MESH)

    def remote(src, dst, send, recv, device):
        return pltpu.make_async_remote_copy(
            src_ref=src, dst_ref=dst, send_sem=send, recv_sem=recv,
            device_id=device, device_id_type=MESH,
        )

    up = {"space": up_sp}
    down = {"space": dn_sp}
    coef_up = remote(craw.at[:, pl.ds(PAD, 8)], craw.at[:, pl.ds(PAD + rows, 8)],
                     halo_send.at[0], halo_recv.at[0], up)
    coef_down = remote(craw.at[:, pl.ds(PAD + rows - 8, 8)], craw.at[:, pl.ds(0, 8)],
                       halo_send.at[1], halo_recv.at[1], down)
    state_up = remote(st.at[pl.ds(PAD, FINE)], st.at[pl.ds(PAD + rows, FINE)],
                      halo_send.at[2], halo_recv.at[2], up)
    state_down = remote(st.at[pl.ds(PAD + rows - FINE, FINE)], st.at[pl.ds(PAD - FINE, FINE)],
                        halo_send.at[3], halo_recv.at[3], down)

    lane = lax.broadcasted_iota(jnp.int32, (8, cols), 1)

    def build(at):
        at = pl.ds(at, 8)
        d = craw[0, at, :] * FINE_DT
        hx = craw[1, at, :] * (0.5 * FINE_DT)
        hy = craw[2, at, :] * (0.5 * FINE_DT)
        parts = [
            -4.0 * d, d + hy, d - hy,
            jnp.where(lane == 0, 0.0, d + hx),
            jnp.where(lane == cols - 1, 0.0, d - hx),
            craw[3, at, :] * FINE_DT, d, d,
        ]
        cf[at] = jnp.swapaxes(jnp.stack(parts, axis=0), 0, 1)

    def prepare(pair):
        for side in (0, 1):
            start_in(pair, side).wait()
            at = block_of(pair, side)
            st[pl.ds(PAD + at, 8)] = jnp.swapaxes(start_ref[:, pl.ds(at, 8), :], 0, 1)
            build(PAD + at if isinstance(pair, int) else pl.multiple_of(PAD + at, 8))

    small[0].wait()
    pick = (lax.broadcasted_iota(jnp.int32, (bands, cols), 1) // (cols // bands)
            == lax.broadcasted_iota(jnp.int32, (bands, cols), 0)).astype(jnp.float32)
    par[...] = jnp.dot(params_ref[...], pick, precision=HIGH, preferred_element_type=jnp.float32)
    pall[me_ens] = params_ref[...]
    for k in range(4):
        coef_in(k).wait()
    prepare(0)

    @pl.when(first)
    def _():
        craw[:, 0:PAD, :] = jnp.zeros((4, PAD, cols), jnp.float32)
        st[0:PAD] = jnp.zeros((PAD, members, cols), jnp.float32)
        rv[0] = jnp.zeros((members, cols), jnp.float32)

    @pl.when(last)
    def _():
        craw[:, PAD + rows:, :] = jnp.zeros((4, PAD, cols), jnp.float32)
        st[PAD + rows:] = jnp.zeros((PAD, members, cols), jnp.float32)
        rv[rows + 1] = jnp.zeros((members, cols), jnp.float32)

    def spread(row, above, middle, below):
        c = [cf[row + PAD, k:k + 1, :] for k in range(5)]
        return (c[0] * middle + c[1] * above + c[2] * below
                + c[3] * pltpu.roll(middle, 1, 1) + c[4] * pltpu.roll(middle, cols - 1, 1))

    def fine(field, row):
        at = row + PAD
        middle = field[at]
        force = cf[at, 5:6, :] * par[...]
        return middle + (spread(row, field[at - 1], middle, field[at + 1]) + force)

    def coarse(row):
        above, middle, below = (rv[row + k] - st[row + PAD - 1 + k] for k in range(3))
        return middle + spread(row, above, middle, below) * float(FINE)

    def row_copy(row):
        return remote(nw.at[row], rv.at[row + 1], row_send.at[row], row_recv.at[row], {"tm": next_tm})

    edge_up = remote(nw.at[0], rv.at[rows + 1], edge_send.at[0], edge_recv.at[0],
                     {"tm": next_tm, "space": up_sp})
    edge_down = remote(nw.at[rows - 1], rv.at[0], edge_send.at[1], edge_recv.at[1],
                       {"tm": next_tm, "space": dn_sp})

    def both(away):
        return half - 1 - away, half + away

    def finish(pair):
        for side in (0, 1):
            at = block_of(pair, side)
            out_ref[:, pl.ds(at, 8), :] = jnp.swapaxes(nw[pl.ds(at, 8)], 0, 1)

    def fine_both(field, away):
        return [fine(field, row) for row in both(away)]

    def keep(field, away, values):
        for row, value in zip(both(away), values):
            field[row + PAD] = value

    @pl.loop(0, FINE - 1)
    def _(t):
        keep(a1, t, fine_both(st, t))
        keep(a2, t - 1, fine_both(a1, t - 1))
        keep(a3, t - 2, fine_both(a2, t - 2))

    pl.semaphore_wait(barrier, len(greeted))
    share_params = remote(params_ref, pall.at[me_ens], ens_send.at[0], ens_recv.at[0], {"ens": other})
    share_params.start()

    @pl.when(jnp.logical_not(first))
    def _():
        coef_up.start()

    @pl.when(jnp.logical_not(last))
    def _():
        coef_down.start()

    @pl.loop(FINE - 1, half + 3)
    def _(t):
        keep(a1, t, fine_both(st, t))
        keep(a2, t - 1, fine_both(a1, t - 1))
        keep(a3, t - 2, fine_both(a2, t - 2))
        q = t - 3

        @pl.when(q >= 0)
        def _():
            upper, lower = both(q)
            values = fine_both(a3, q)
            nw[upper] = values[0]
            nw[lower] = values[1]

            @pl.when(receives)
            def _():
                @pl.when(q == 0)
                def _():
                    row_copy(half - 1).wait_recv()
                    row_copy(half).wait_recv()

                @pl.when(q < half - 1)
                def _():
                    row_copy(upper - 1).wait_recv()
                    row_copy(lower + 1).wait_recv()

                @pl.when(q == half - 1)
                def _():
                    @pl.when(jnp.logical_not(last))
                    def _():
                        edge_up.wait_recv()

                    @pl.when(jnp.logical_not(first))
                    def _():
                        edge_down.wait_recv()

                more = [coarse(upper), coarse(lower)]
                nw[upper] = nw[upper] + more[0]
                nw[lower] = nw[lower] + more[1]

            @pl.when(sends)
            def _():
                @pl.when(q == half - 1)
                def _():
                    @pl.when(jnp.logical_not(first))
                    def _():
                        edge_up.start()

                    @pl.when(jnp.logical_not(last))
                    def _():
                        edge_down.start()

                @pl.when(q >= AHEAD)
                def _():
                    row_copy(upper + AHEAD).wait_send()
                    row_copy(lower - AHEAD).wait_send()

                row_copy(upper).start()
                row_copy(lower).start()

            @pl.when(jnp.logical_and(lax.rem(q, 8) == 7, q < half - 1))
            def _():
                finish(q // 8)

        @pl.when(jnp.logical_and(lax.rem(t, 8) == 6, t < half - 2))
        def _():
            prepare((t + 2) // 8)

        @pl.when(t == half - 9)
        def _():
            @pl.when(jnp.logical_not(first))
            def _():
                state_up.start()

            @pl.when(jnp.logical_not(last))
            def _():
                state_down.start()

        @pl.when(t == half - 2)
        def _():
            @pl.when(jnp.logical_not(last))
            def _():
                coef_up.wait_recv()
                state_up.wait_recv()

            @pl.when(jnp.logical_not(first))
            def _():
                coef_down.wait_recv()
                state_down.wait_recv()

            build(0)
            build(PAD + rows)

    for copy in small[1:]:
        copy.wait()
    mine = (lax.broadcasted_iota(jnp.int32, (members, members * n_ens), 1)
            == lax.broadcasted_iota(jnp.int32, (members, members * n_ens), 0) + me_ens * members)
    noise = lax.dot_general(mine.astype(jnp.float32), noise_ref[...], (((1,), (0,)), ((), ())),
                            precision=HIGH, preferred_element_type=jnp.float32)
    target = data_ref[...] + noise
    inv_spread = lax.rsqrt(var_ref[...])

    lanes = lax.broadcasted_iota(jnp.int32, (members, 128), 1)
    wide = lax.broadcasted_iota(jnp.int32, (members, cols), 1)

    def gather(o, found):
        cell = lax.rem(cell_ref[0, o], rows * cols)
        row = lax.div(cell, cols)
        col = lax.rem(cell, cols)
        value = jnp.sum(jnp.where(wide == col, nw[row], 0.0), axis=1, keepdims=True)
        return jnp.where(lanes == o, value, found)

    found = lax.fori_loop(0, n_obs, gather, jnp.zeros((members, 128), jnp.float32), unroll=8)
    predicted = found[:, :n_obs]
    xall[me_ens] = jnp.concatenate(
        [predicted * inv_spread, (target - predicted) * inv_spread], axis=1)
    share_pred = remote(xall.at[me_ens], xall.at[me_ens], ens_send.at[1], ens_recv.at[1], {"ens": other})
    share_pred.start()

    finish(pairs - 1)
    share_pred.wait()
    total = members * n_ens
    norm_factor = 1.0 / math.sqrt(total - 1)
    everyone = jnp.concatenate([xall[e] for e in range(n_ens)], axis=0)
    scaled, misfit = everyone[:, :n_obs], everyone[:, n_obs:]
    anomaly = (scaled - jnp.mean(scaled, axis=0, keepdims=True)) * norm_factor
    here = me_tm * n_sp + me_sp
    right = jnp.concatenate(
        [anomaly, misfit, jnp.zeros((128 - 2 * total, n_obs), jnp.float32)], axis=0)
    sums[here] = lax.dot_general(anomaly, right, NT, precision=HIGH,
                                 preferred_element_type=jnp.float32)

    def sum_copy(slot, t, z):
        return remote(sums.at[slot], sums.at[slot], sum_send.at[t * n_sp + z], sum_recv.at[slot],
                      {"tm": t, "space": z})

    for t, z in chips:
        sum_copy(here, t, z).start()
    for t, z in chips:
        sum_copy(t * n_sp + z, t, z).wait_recv()
    system = jnp.sum(sums[...], axis=0)

    row_no = lax.broadcasted_iota(jnp.int32, (total, 128), 0)
    system = system + (row_no == lax.broadcasted_iota(jnp.int32, (total, 128), 1)).astype(jnp.float32)
    for k in range(total):
        pivot_row = system[k:k + 1, :] / system[k:k + 1, k:k + 1]
        system = jnp.where(row_no == k, pivot_row, system - system[:, k:k + 1] * pivot_row)
    weights = system[:, total:2 * total]

    share_params.wait()
    every_param = jnp.concatenate([pall[e] for e in range(n_ens)], axis=0)
    param_anom = every_param - jnp.mean(every_param, axis=0, keepdims=True)
    update = lax.dot_general(weights, param_anom, TN, precision=HIGH,
                             preferred_element_type=jnp.float32) * norm_factor
    own = jnp.where(me_ens == 0, update[:members], update[members:])
    new_params_ref[...] = params_ref[...] + own

    @pl.when(jnp.logical_not(first))
    def _():
        coef_up.wait_send()
        state_up.wait_send()

    @pl.when(jnp.logical_not(last))
    def _():
        coef_down.wait_send()
        state_down.wait_send()

    @pl.when(sends)
    def _():
        @pl.when(jnp.logical_not(first))
        def _():
            edge_up.wait_send()

        @pl.when(jnp.logical_not(last))
        def _():
            edge_down.wait_send()

        for row in (*range(AHEAD), *range(rows - AHEAD, rows)):
            row_copy(row).wait_send()

    for t, z in chips:
        sum_copy(here, t, z).wait_send()


def per_device(sizes, start_states, velocity_x, velocity_y, diffusivity, source_shape, params,
               obs_cell, obs_data, obs_noise, obs_var):
    state = start_states[0]
    members, rows, cols = state.shape
    n_tm, n_sp, n_ens = sizes
    total = members * n_ens
    padded = (rows + 2 * PAD, members, cols)
    f32 = jnp.float32
    vmem = pl.BlockSpec(memory_space=pltpu.VMEM)
    hbm = pl.BlockSpec(memory_space=pl.ANY)
    dma = pltpu.SemaphoreType.DMA
    pairs = rows // 16
    new_states, new_params = pl.pallas_call(
        functools.partial(kernel, sizes),
        out_shape=(jax.ShapeDtypeStruct(state.shape, f32), jax.ShapeDtypeStruct(params.shape, f32)),
        in_specs=[hbm] * 10,
        out_specs=(vmem, vmem),
        scratch_shapes=[
            pltpu.VMEM(state.shape, f32),
            pltpu.VMEM(params.shape, f32),
            pltpu.SMEM(obs_cell.shape, jnp.int32),
            pltpu.VMEM(obs_data.shape, f32),
            pltpu.VMEM((total, obs_data.shape[1]), f32),
            pltpu.VMEM(obs_var.shape, f32),
            pltpu.VMEM(padded, f32),
            pltpu.VMEM(padded, f32),
            pltpu.VMEM(padded, f32),
            pltpu.VMEM(padded, f32),
            pltpu.VMEM((rows, members, cols), f32),
            pltpu.VMEM((rows + 2, members, cols), f32),
            pltpu.VMEM((4, rows + 2 * PAD, cols), f32),
            pltpu.VMEM((rows + 2 * PAD, 8, cols), f32),
            pltpu.VMEM((members, cols), f32),
            pltpu.VMEM((n_ens,) + params.shape, f32),
            pltpu.VMEM((n_ens, members, 128), f32),
            pltpu.VMEM((n_tm * n_sp, total, 128), f32),
            dma((4,)), dma((5,)), dma((2, pairs)),
            dma((4,)), dma((4,)),
            dma((rows,)), dma((rows,)),
            dma((2,)), dma((2,)),
            dma((2,)), dma((2,)),
            dma((n_tm * n_sp,)), dma((n_tm * n_sp,)),
        ],
        compiler_params=pltpu.CompilerParams(
            collective_id=0, has_side_effects=True, vmem_limit_bytes=60 * 2**20
        ),
    )(state, velocity_x, velocity_y, diffusivity, source_shape, params,
      obs_cell, obs_data, jnp.swapaxes(obs_noise[0], 0, 1), obs_var)
    return (new_states[None], new_params)


def solution(mesh):
    sizes = tuple(mesh.shape[axis] for axis in ("tm", "space", "ens"))
    in_specs = (
        P("tm", "ens", "space", None),
        P("space", None),
        P("space", None),
        P("space", None),
        P("space", None),
        P("ens", None),
        P("tm", "space"),
        P("tm", "space"),
        P("tm", "space", None),
        P("tm", "space"),
    )
    out_specs = (P("tm", "ens", "space", None), P("ens", None))
    return jax.shard_map(
        functools.partial(per_device, sizes), mesh=mesh,
        in_specs=in_specs, out_specs=out_specs, check_vma=False,
    )
```

```python
import functools
import math

import jax
import jax.numpy as jnp
from jax import lax
from jax.experimental import pallas as pl
from jax.experimental.pallas import tpu as pltpu
from jax.sharding import PartitionSpec as P

FINE = 4
FINE_DT = 0.25
PAD = 8
AHEAD = 3
MESH = pl.DeviceIdType.MESH
HIGH = lax.Precision.HIGHEST
NT = (((1,), (1,)), ((), ()))
TN = (((0,), (0,)), ((), ()))


def kernel(
    sizes,
    start_hbm, vx_hbm, vy_hbm, diff_hbm, src_hbm, params_hbm,
    cell_hbm, data_hbm, noise_hbm, var_hbm,
    out_ref, new_params_ref,
    start_ref, params_ref, cell_ref, data_ref, noise_ref, var_ref,
    st, a1, a2, a3, nw, rv, craw, cf, par, pall, xall, sums,
    in_sem, small_sem, block_sem,
    halo_send, halo_recv, row_send, row_recv, edge_send, edge_recv,
    ens_send, ens_recv, sum_send, sum_recv,
):
    n_tm, n_sp, n_ens = sizes
    me_tm = lax.axis_index("tm")
    me_sp = lax.axis_index("space")
    me_ens = lax.axis_index("ens")
    members, rows, cols = start_ref.shape
    half = rows // 2
    pairs = half // 8
    bands = params_ref.shape[1]
    n_obs = data_ref.shape[1]
    other = 1 - me_ens
    first, last = me_sp == 0, me_sp == n_sp - 1
    up_sp = lax.rem(me_sp + n_sp - 1, n_sp)
    dn_sp = lax.rem(me_sp + 1, n_sp)
    next_tm = lax.rem(me_tm + 1, n_tm)
    sends = me_tm < n_tm - 1
    receives = me_tm > 0

    def block_of(pair, side):
        at = half - 8 - 8 * pair if side == 0 else half + 8 * pair
        return at if isinstance(pair, int) else pl.multiple_of(at, 8)

    def start_in(pair, side):
        at = pl.ds(block_of(pair, side), 8)
        return pltpu.make_async_copy(start_hbm.at[:, at], start_ref.at[:, at], block_sem.at[side, pair])

    def coef_in(k):
        ref = (diff_hbm, vx_hbm, vy_hbm, src_hbm)[k]
        return pltpu.make_async_copy(ref, craw.at[k, pl.ds(PAD, rows)], in_sem.at[k])

    small = [
        pltpu.make_async_copy(src, dst, small_sem.at[k])
        for k, (src, dst) in enumerate((
            (params_hbm, params_ref), (cell_hbm, cell_ref), (data_hbm, data_ref),
            (noise_hbm, noise_ref), (var_hbm, var_ref)))
    ]
    start_in(0, 0).start()
    start_in(0, 1).start()
    for k in range(4):
        coef_in(k).start()
    for copy in small:
        copy.start()
    for pair in range(1, pairs):
        start_in(pair, 0).start()
        start_in(pair, 1).start()

    barrier = pltpu.get_barrier_semaphore()
    chips = [(lax.rem(me_tm + t, n_tm), lax.rem(me_sp + z, n_sp))
             for t in range(n_tm) for z in range(n_sp) if t or z]
    greeted = [{"ens": other}] + [{"tm": t, "space": z} for t, z in chips]
    for device in greeted:
        pl.semaphore_signal(barrier, inc=1, device_id=device, device_id_type=MESH)

    def remote(src, dst, send, recv, device):
        return pltpu.make_async_remote_copy(
            src_ref=src, dst_ref=dst, send_sem=send, recv_sem=recv,
            device_id=device, device_id_type=MESH,
        )

    up = {"space": up_sp}
    down = {"space": dn_sp}
    coef_up = remote(craw.at[:, pl.ds(PAD, 8)], craw.at[:, pl.ds(PAD + rows, 8)],
                     halo_send.at[0], halo_recv.at[0], up)
    coef_down = remote(craw.at[:, pl.ds(PAD + rows - 8, 8)], craw.at[:, pl.ds(0, 8)],
                       halo_send.at[1], halo_recv.at[1], down)
    state_up = remote(st.at[pl.ds(PAD, FINE)], st.at[pl.ds(PAD + rows, FINE)],
                      halo_send.at[2], halo_recv.at[2], up)
    state_down = remote(st.at[pl.ds(PAD + rows - FINE, FINE)], st.at[pl.ds(PAD - FINE, FINE)],
                        halo_send.at[3], halo_recv.at[3], down)

    lane = lax.broadcasted_iota(jnp.int32, (8, cols), 1)

    def build(at):
        at = pl.ds(at, 8)
        d = craw[0, at, :] * FINE_DT
        hx = craw[1, at, :] * (0.5 * FINE_DT)
        hy = craw[2, at, :] * (0.5 * FINE_DT)
        parts = [
            -4.0 * d, d + hy, d - hy,
            jnp.where(lane == 0, 0.0, d + hx),
            jnp.where(lane == cols - 1, 0.0, d - hx),
            craw[3, at, :] * FINE_DT, d, d,
        ]
        cf[at] = jnp.swapaxes(jnp.stack(parts, axis=0), 0, 1)

    def prepare(pair):
        for side in (0, 1):
            start_in(pair, side).wait()
            at = block_of(pair, side)
            st[pl.ds(PAD + at, 8)] = jnp.swapaxes(start_ref[:, pl.ds(at, 8), :], 0, 1)
            build(PAD + at if isinstance(pair, int) else pl.multiple_of(PAD + at, 8))

    small[0].wait()
    pick = (lax.broadcasted_iota(jnp.int32, (bands, cols), 1) // (cols // bands)
            == lax.broadcasted_iota(jnp.int32, (bands, cols), 0)).astype(jnp.float32)
    par[...] = jnp.dot(params_ref[...], pick, precision=HIGH, preferred_element_type=jnp.float32)
    pall[me_ens] = params_ref[...]
    for k in range(4):
        coef_in(k).wait()
    prepare(0)

    @pl.when(first)
    def _():
        craw[:, 0:PAD, :] = jnp.zeros((4, PAD, cols), jnp.float32)
        st[0:PAD] = jnp.zeros((PAD, members, cols), jnp.float32)
        rv[0] = jnp.zeros((members, cols), jnp.float32)

    @pl.when(last)
    def _():
        craw[:, PAD + rows:, :] = jnp.zeros((4, PAD, cols), jnp.float32)
        st[PAD + rows:] = jnp.zeros((PAD, members, cols), jnp.float32)
        rv[rows + 1] = jnp.zeros((members, cols), jnp.float32)

    def spread(row, above, middle, below):
        c = [cf[row + PAD, k:k + 1, :] for k in range(5)]
        return (c[0] * middle + c[1] * above + c[2] * below
                + c[3] * pltpu.roll(middle, 1, 1) + c[4] * pltpu.roll(middle, cols - 1, 1))

    def fine(field, row):
        at = row + PAD
        middle = field[at]
        force = cf[at, 5:6, :] * par[...]
        return middle + (spread(row, field[at - 1], middle, field[at + 1]) + force)

    def coarse(row):
        above, middle, below = (rv[row + k] - st[row + PAD - 1 + k] for k in range(3))
        return middle + spread(row, above, middle, below) * float(FINE)

    def row_copy(row):
        return remote(nw.at[row], rv.at[row + 1], row_send.at[row], row_recv.at[row], {"tm": next_tm})

    edge_up = remote(nw.at[0], rv.at[rows + 1], edge_send.at[0], edge_recv.at[0],
                     {"tm": next_tm, "space": up_sp})
    edge_down = remote(nw.at[rows - 1], rv.at[0], edge_send.at[1], edge_recv.at[1],
                       {"tm": next_tm, "space": dn_sp})

    def both(away):
        return half - 1 - away, half + away

    def finish(pair):
        for side in (0, 1):
            at = block_of(pair, side)
            out_ref[:, pl.ds(at, 8), :] = jnp.swapaxes(nw[pl.ds(at, 8)], 0, 1)

    def fine_both(field, away):
        return [fine(field, row) for row in both(away)]

    def keep(field, away, values):
        for row, value in zip(both(away), values):
            field[row + PAD] = value

    fields = (st, a1, a2, a3)

    def fine_steps(t, count):
        for k in reversed(range(count)):
            keep(fields[k + 1], t - 2 * k, fine_both(fields[k], t - 2 * k))

    for count in range(1, FINE):
        @pl.loop(2 * count - 2, 2 * count)
        def _(t):
            fine_steps(t, count)

    pl.semaphore_wait(barrier, len(greeted))
    share_params = remote(params_ref, pall.at[me_ens], ens_send.at[0], ens_recv.at[0], {"ens": other})
    share_params.start()

    @pl.when(jnp.logical_not(first))
    def _():
        coef_up.start()

    @pl.when(jnp.logical_not(last))
    def _():
        coef_down.start()

    for copy in small[1:]:
        copy.wait()
    mine = (lax.broadcasted_iota(jnp.int32, (members, members * n_ens), 1)
            == lax.broadcasted_iota(jnp.int32, (members, members * n_ens), 0) + me_ens * members)
    noise = lax.dot_general(mine.astype(jnp.float32), noise_ref[...], (((1,), (0,)), ((), ())),
                            precision=HIGH, preferred_element_type=jnp.float32)
    target = data_ref[...] + noise
    inv_spread = lax.rsqrt(var_ref[...])

    delay = 2 * (FINE - 1)

    @pl.loop(delay, half + delay)
    def _(t):
        q = t - delay
        upper, lower = both(q)
        values = fine_both(a3, q)
        nw[upper] = values[0]
        nw[lower] = values[1]
        fine_steps(t, FINE - 1)

        @pl.when(receives)
        def _():
            @pl.when(q == 0)
            def _():
                row_copy(half - 1).wait_recv()
                row_copy(half).wait_recv()

            @pl.when(q < half - 1)
            def _():
                row_copy(upper - 1).wait_recv()
                row_copy(lower + 1).wait_recv()

            @pl.when(q == half - 1)
            def _():
                @pl.when(jnp.logical_not(last))
                def _():
                    edge_up.wait_recv()

                @pl.when(jnp.logical_not(first))
                def _():
                    edge_down.wait_recv()

            more = [coarse(upper), coarse(lower)]
            nw[upper] = nw[upper] + more[0]
            nw[lower] = nw[lower] + more[1]

        @pl.when(sends)
        def _():
            @pl.when(q == half - 1)
            def _():
                @pl.when(jnp.logical_not(first))
                def _():
                    edge_up.start()

                @pl.when(jnp.logical_not(last))
                def _():
                    edge_down.start()

            @pl.when(q >= AHEAD)
            def _():
                row_copy(upper + AHEAD).wait_send()
                row_copy(lower - AHEAD).wait_send()

            row_copy(upper).start()
            row_copy(lower).start()

        @pl.when(jnp.logical_and(lax.rem(q, 8) == 7, q < half - 1))
        def _():
            finish(q // 8)

        @pl.when(jnp.logical_and(lax.rem(t, 8) == 6, t < half - 2))
        def _():
            prepare((t + 2) // 8)

        @pl.when(t == half - 9)
        def _():
            @pl.when(jnp.logical_not(first))
            def _():
                state_up.start()

            @pl.when(jnp.logical_not(last))
            def _():
                state_down.start()

        @pl.when(t == half - 2)
        def _():
            @pl.when(jnp.logical_not(last))
            def _():
                coef_up.wait_recv()
                state_up.wait_recv()

            @pl.when(jnp.logical_not(first))
            def _():
                coef_down.wait_recv()
                state_down.wait_recv()

            build(0)
            build(PAD + rows)

    lanes = lax.broadcasted_iota(jnp.int32, (members, 128), 1)
    wide = lax.broadcasted_iota(jnp.int32, (members, cols), 1)

    def gather(o, found):
        cell = lax.rem(cell_ref[0, o], rows * cols)
        row = lax.div(cell, cols)
        col = lax.rem(cell, cols)
        value = jnp.sum(jnp.where(wide == col, nw[row], 0.0), axis=1, keepdims=True)
        return jnp.where(lanes == o, value, found)

    found = lax.fori_loop(0, n_obs, gather, jnp.zeros((members, 128), jnp.float32), unroll=8)
    predicted = found[:, :n_obs]
    xall[me_ens] = jnp.concatenate(
        [predicted * inv_spread, (target - predicted) * inv_spread], axis=1)
    share_pred = remote(xall.at[me_ens], xall.at[me_ens], ens_send.at[1], ens_recv.at[1], {"ens": other})
    share_pred.start()

    finish(pairs - 1)
    share_pred.wait()
    total = members * n_ens
    norm_factor = 1.0 / math.sqrt(total - 1)
    everyone = jnp.concatenate([xall[e] for e in range(n_ens)], axis=0)
    scaled, misfit = everyone[:, :n_obs], everyone[:, n_obs:]
    anomaly = (scaled - jnp.mean(scaled, axis=0, keepdims=True)) * norm_factor
    here = me_tm * n_sp + me_sp
    right = jnp.concatenate(
        [anomaly, misfit, jnp.zeros((128 - 2 * total, n_obs), jnp.float32)], axis=0)
    sums[here] = lax.dot_general(anomaly, right, NT, precision=HIGH,
                                 preferred_element_type=jnp.float32)

    def sum_copy(slot, t, z):
        return remote(sums.at[slot], sums.at[slot], sum_send.at[t * n_sp + z], sum_recv.at[slot],
                      {"tm": t, "space": z})

    for t, z in chips:
        sum_copy(here, t, z).start()
    for t, z in chips:
        sum_copy(t * n_sp + z, t, z).wait_recv()
    system = jnp.sum(sums[...], axis=0)

    row_no = lax.broadcasted_iota(jnp.int32, (total, 128), 0)
    system = system + (row_no == lax.broadcasted_iota(jnp.int32, (total, 128), 1)).astype(jnp.float32)
    for k in range(total):
        pivot_row = system[k:k + 1, :] / system[k:k + 1, k:k + 1]
        system = jnp.where(row_no == k, pivot_row, system - system[:, k:k + 1] * pivot_row)
    weights = system[:, total:2 * total]

    share_params.wait()
    every_param = jnp.concatenate([pall[e] for e in range(n_ens)], axis=0)
    param_anom = every_param - jnp.mean(every_param, axis=0, keepdims=True)
    update = lax.dot_general(weights, param_anom, TN, precision=HIGH,
                             preferred_element_type=jnp.float32) * norm_factor
    own = jnp.where(me_ens == 0, update[:members], update[members:])
    new_params_ref[...] = params_ref[...] + own

    @pl.when(jnp.logical_not(first))
    def _():
        coef_up.wait_send()
        state_up.wait_send()

    @pl.when(jnp.logical_not(last))
    def _():
        coef_down.wait_send()
        state_down.wait_send()

    @pl.when(sends)
    def _():
        @pl.when(jnp.logical_not(first))
        def _():
            edge_up.wait_send()

        @pl.when(jnp.logical_not(last))
        def _():
            edge_down.wait_send()

        for row in (*range(AHEAD), *range(rows - AHEAD, rows)):
            row_copy(row).wait_send()

    for t, z in chips:
        sum_copy(here, t, z).wait_send()


def per_device(sizes, start_states, velocity_x, velocity_y, diffusivity, source_shape, params,
               obs_cell, obs_data, obs_noise, obs_var):
    state = start_states[0]
    members, rows, cols = state.shape
    n_tm, n_sp, n_ens = sizes
    total = members * n_ens
    padded = (rows + 2 * PAD, members, cols)
    f32 = jnp.float32
    vmem = pl.BlockSpec(memory_space=pltpu.VMEM)
    hbm = pl.BlockSpec(memory_space=pl.ANY)
    dma = pltpu.SemaphoreType.DMA
    pairs = rows // 16
    new_states, new_params = pl.pallas_call(
        functools.partial(kernel, sizes),
        out_shape=(jax.ShapeDtypeStruct(state.shape, f32), jax.ShapeDtypeStruct(params.shape, f32)),
        in_specs=[hbm] * 10,
        out_specs=(vmem, vmem),
        scratch_shapes=[
            pltpu.VMEM(state.shape, f32),
            pltpu.VMEM(params.shape, f32),
            pltpu.SMEM(obs_cell.shape, jnp.int32),
            pltpu.VMEM(obs_data.shape, f32),
            pltpu.VMEM((total, obs_data.shape[1]), f32),
            pltpu.VMEM(obs_var.shape, f32),
            pltpu.VMEM(padded, f32),
            pltpu.VMEM(padded, f32),
            pltpu.VMEM(padded, f32),
            pltpu.VMEM(padded, f32),
            pltpu.VMEM((rows, members, cols), f32),
            pltpu.VMEM((rows + 2, members, cols), f32),
            pltpu.VMEM((4, rows + 2 * PAD, cols), f32),
            pltpu.VMEM((rows + 2 * PAD, 8, cols), f32),
            pltpu.VMEM((members, cols), f32),
            pltpu.VMEM((n_ens,) + params.shape, f32),
            pltpu.VMEM((n_ens, members, 128), f32),
            pltpu.VMEM((n_tm * n_sp, total, 128), f32),
            dma((4,)), dma((5,)), dma((2, pairs)),
            dma((4,)), dma((4,)),
            dma((rows,)), dma((rows,)),
            dma((2,)), dma((2,)),
            dma((2,)), dma((2,)),
            dma((n_tm * n_sp,)), dma((n_tm * n_sp,)),
        ],
        compiler_params=pltpu.CompilerParams(
            collective_id=0, has_side_effects=True, vmem_limit_bytes=60 * 2**20
        ),
    )(state, velocity_x, velocity_y, diffusivity, source_shape, params,
      obs_cell, obs_data, jnp.swapaxes(obs_noise[0], 0, 1), obs_var)
    return (new_states[None], new_params)


def solution(mesh):
    sizes = tuple(mesh.shape[axis] for axis in ("tm", "space", "ens"))
    in_specs = (
        P("tm", "ens", "space", None),
        P("space", None),
        P("space", None),
        P("space", None),
        P("space", None),
        P("ens", None),
        P("tm", "space"),
        P("tm", "space"),
        P("tm", "space", None),
        P("tm", "space"),
    )
    out_specs = (P("tm", "ens", "space", None), P("ens", None))
    return jax.shard_map(
        functools.partial(per_device, sizes), mesh=mesh,
        in_specs=in_specs, out_specs=out_specs, check_vma=False,
    )
```

```python
import functools
import math

import jax
import jax.numpy as jnp
from jax import lax
from jax.experimental import pallas as pl
from jax.experimental.pallas import tpu as pltpu
from jax.sharding import PartitionSpec as P

FINE = 4
FINE_DT = 0.25
PAD = 8
AHEAD = 8
MESH = pl.DeviceIdType.MESH
HIGH = lax.Precision.HIGHEST
NT = (((1,), (1,)), ((), ()))
TN = (((0,), (0,)), ((), ()))


def kernel(
    sizes,
    start_hbm, vx_hbm, vy_hbm, diff_hbm, src_hbm, params_hbm,
    cell_hbm, data_hbm, noise_hbm, var_hbm,
    out_ref, new_params_ref,
    start_ref, params_ref, cell_ref, data_ref, noise_ref, var_ref,
    st, a1, a2, a3, nw, rv, craw, cf, par, pall, xall, sums,
    in_sem, small_sem, block_sem,
    halo_send, halo_recv, row_send, row_recv, edge_send, edge_recv,
    ens_send, ens_recv, sum_send, sum_recv,
):
    n_tm, n_sp, n_ens = sizes
    me_tm = lax.axis_index("tm")
    me_sp = lax.axis_index("space")
    me_ens = lax.axis_index("ens")
    members, rows, cols = start_ref.shape
    half = rows // 2
    pairs = half // 8
    bands = params_ref.shape[1]
    n_obs = data_ref.shape[1]
    other = 1 - me_ens
    first, last = me_sp == 0, me_sp == n_sp - 1
    up_sp = lax.rem(me_sp + n_sp - 1, n_sp)
    dn_sp = lax.rem(me_sp + 1, n_sp)
    next_tm = lax.rem(me_tm + 1, n_tm)
    sends = me_tm < n_tm - 1
    receives = me_tm > 0

    def block_of(pair, side):
        at = half - 8 - 8 * pair if side == 0 else half + 8 * pair
        return at if isinstance(pair, int) else pl.multiple_of(at, 8)

    def start_in(pair, side):
        at = pl.ds(block_of(pair, side), 8)
        return pltpu.make_async_copy(start_hbm.at[:, at], start_ref.at[:, at], block_sem.at[side, pair])

    def coef_in(k):
        ref = (diff_hbm, vx_hbm, vy_hbm, src_hbm)[k]
        return pltpu.make_async_copy(ref, craw.at[k, pl.ds(PAD, rows)], in_sem.at[k])

    small = [
        pltpu.make_async_copy(src, dst, small_sem.at[k])
        for k, (src, dst) in enumerate((
            (params_hbm, params_ref), (cell_hbm, cell_ref), (data_hbm, data_ref),
            (noise_hbm, noise_ref), (var_hbm, var_ref)))
    ]
    start_in(0, 0).start()
    start_in(0, 1).start()
    for k in range(4):
        coef_in(k).start()
    for copy in small:
        copy.start()
    for pair in range(1, pairs):
        start_in(pair, 0).start()
        start_in(pair, 1).start()

    barrier = pltpu.get_barrier_semaphore()
    chips = [(lax.rem(me_tm + t, n_tm), lax.rem(me_sp + z, n_sp))
             for t in range(n_tm) for z in range(n_sp) if t or z]
    greeted = [{"ens": other}] + [{"tm": t, "space": z} for t, z in chips]
    for device in greeted:
        pl.semaphore_signal(barrier, inc=1, device_id=device, device_id_type=MESH)

    def remote(src, dst, send, recv, device):
        return pltpu.make_async_remote_copy(
            src_ref=src, dst_ref=dst, send_sem=send, recv_sem=recv,
            device_id=device, device_id_type=MESH,
        )

    up = {"space": up_sp}
    down = {"space": dn_sp}
    coef_up = remote(craw.at[:, pl.ds(PAD, 8)], craw.at[:, pl.ds(PAD + rows, 8)],
                     halo_send.at[0], halo_recv.at[0], up)
    coef_down = remote(craw.at[:, pl.ds(PAD + rows - 8, 8)], craw.at[:, pl.ds(0, 8)],
                       halo_send.at[1], halo_recv.at[1], down)
    state_up = remote(st.at[pl.ds(PAD, FINE)], st.at[pl.ds(PAD + rows, FINE)],
                      halo_send.at[2], halo_recv.at[2], up)
    state_down = remote(st.at[pl.ds(PAD + rows - FINE, FINE)], st.at[pl.ds(PAD - FINE, FINE)],
                        halo_send.at[3], halo_recv.at[3], down)

    lane = lax.broadcasted_iota(jnp.int32, (8, cols), 1)

    def build(at):
        rows_at = pl.ds(at, 8)
        d = craw[0, rows_at, :] * FINE_DT
        hx = craw[1, rows_at, :] * (0.5 * FINE_DT)
        hy = craw[2, rows_at, :] * (0.5 * FINE_DT)
        parts = [
            -4.0 * d, d + hy, d - hy,
            jnp.where(lane == 0, 0.0, d + hx),
            jnp.where(lane == cols - 1, 0.0, d - hx),
            craw[3, rows_at, :] * FINE_DT,
        ]
        for i in range(8):
            for k, part in enumerate(parts):
                spread_out = jnp.broadcast_to(part[i:i + 1, :], (members, cols))
                cf[at + i, k] = spread_out * par[...] if k == 5 else spread_out

    def prepare(pair):
        for side in (0, 1):
            start_in(pair, side).wait()
            at = block_of(pair, side)
            st[pl.ds(PAD + at, 8)] = jnp.swapaxes(start_ref[:, pl.ds(at, 8), :], 0, 1)
            build(PAD + at if isinstance(pair, int) else pl.multiple_of(PAD + at, 8))

    small[0].wait()
    pick = (lax.broadcasted_iota(jnp.int32, (bands, cols), 1) // (cols // bands)
            == lax.broadcasted_iota(jnp.int32, (bands, cols), 0)).astype(jnp.float32)
    par[...] = jnp.dot(params_ref[...], pick, precision=HIGH, preferred_element_type=jnp.float32)
    pall[me_ens] = params_ref[...]
    for k in range(4):
        coef_in(k).wait()
    prepare(0)

    @pl.when(first)
    def _():
        craw[:, 0:PAD, :] = jnp.zeros((4, PAD, cols), jnp.float32)
        st[0:PAD] = jnp.zeros((PAD, members, cols), jnp.float32)
        rv[0] = jnp.zeros((members, cols), jnp.float32)

    @pl.when(last)
    def _():
        craw[:, PAD + rows:, :] = jnp.zeros((4, PAD, cols), jnp.float32)
        st[PAD + rows:] = jnp.zeros((PAD, members, cols), jnp.float32)
        rv[rows + 1] = jnp.zeros((members, cols), jnp.float32)

    def spread(row, above, middle, below):
        c = [cf[row + PAD, k] for k in range(5)]
        return (c[0] * middle + c[1] * above + c[2] * below
                + c[3] * pltpu.roll(middle, 1, 1) + c[4] * pltpu.roll(middle, cols - 1, 1))

    def fine(field, row):
        at = row + PAD
        middle = field[at]
        return middle + (spread(row, field[at - 1], middle, field[at + 1]) + cf[at, 5])

    def coarse(row):
        above, middle, below = (rv[row + k] - st[row + PAD - 1 + k] for k in range(3))
        return middle + spread(row, above, middle, below) * float(FINE)

    def row_copy(row):
        return remote(nw.at[row], rv.at[row + 1], row_send.at[row], row_recv.at[row], {"tm": next_tm})

    edge_up = remote(nw.at[0], rv.at[rows + 1], edge_send.at[0], edge_recv.at[0],
                     {"tm": next_tm, "space": up_sp})
    edge_down = remote(nw.at[rows - 1], rv.at[0], edge_send.at[1], edge_recv.at[1],
                       {"tm": next_tm, "space": dn_sp})

    def both(away):
        return half - 1 - away, half + away

    def finish(pair):
        for side in (0, 1):
            at = block_of(pair, side)
            out_ref[:, pl.ds(at, 8), :] = jnp.swapaxes(nw[pl.ds(at, 8)], 0, 1)

    def fine_both(field, away):
        return [fine(field, row) for row in both(away)]

    def keep(field, away, values):
        for row, value in zip(both(away), values):
            field[row + PAD] = value

    fields = (st, a1, a2, a3)

    def fine_steps(t, count):
        for k in reversed(range(count)):
            keep(fields[k + 1], t - 2 * k, fine_both(fields[k], t - 2 * k))

    for count in range(1, FINE):
        @pl.loop(2 * count - 2, 2 * count)
        def _(t):
            fine_steps(t, count)

    pl.semaphore_wait(barrier, len(greeted))
    share_params = remote(params_ref, pall.at[me_ens], ens_send.at[0], ens_recv.at[0], {"ens": other})
    share_params.start()

    @pl.when(jnp.logical_not(first))
    def _():
        coef_up.start()

    @pl.when(jnp.logical_not(last))
    def _():
        coef_down.start()

    for copy in small[1:]:
        copy.wait()
    mine = (lax.broadcasted_iota(jnp.int32, (members, members * n_ens), 1)
            == lax.broadcasted_iota(jnp.int32, (members, members * n_ens), 0) + me_ens * members)
    noise = lax.dot_general(mine.astype(jnp.float32), noise_ref[...], (((1,), (0,)), ((), ())),
                            precision=HIGH, preferred_element_type=jnp.float32)
    target = data_ref[...] + noise
    inv_spread = lax.rsqrt(var_ref[...])

    delay = 2 * (FINE - 1)

    @pl.loop(delay, half + delay)
    def _(t):
        q = t - delay
        upper, lower = both(q)
        values = fine_both(a3, q)
        nw[upper] = values[0]
        nw[lower] = values[1]
        fine_steps(t, FINE - 1)

        @pl.when(receives)
        def _():
            @pl.when(q == 0)
            def _():
                row_copy(half - 1).wait_recv()
                row_copy(half).wait_recv()

            @pl.when(q < half - 1)
            def _():
                row_copy(upper - 1).wait_recv()
                row_copy(lower + 1).wait_recv()

            @pl.when(q == half - 1)
            def _():
                @pl.when(jnp.logical_not(last))
                def _():
                    edge_up.wait_recv()

                @pl.when(jnp.logical_not(first))
                def _():
                    edge_down.wait_recv()

            more = [coarse(upper), coarse(lower)]
            nw[upper] = nw[upper] + more[0]
            nw[lower] = nw[lower] + more[1]

        @pl.when(sends)
        def _():
            @pl.when(q == half - 1)
            def _():
                @pl.when(jnp.logical_not(first))
                def _():
                    edge_up.start()

                @pl.when(jnp.logical_not(last))
                def _():
                    edge_down.start()

            @pl.when(q >= AHEAD)
            def _():
                row_copy(upper + AHEAD).wait_send()
                row_copy(lower - AHEAD).wait_send()

            row_copy(upper).start()
            row_copy(lower).start()

        @pl.when(jnp.logical_and(lax.rem(q, 8) == 7, q < half - 1))
        def _():
            finish(q // 8)

        @pl.when(jnp.logical_and(lax.rem(t, 8) == 6, t < half - 2))
        def _():
            prepare((t + 2) // 8)

        @pl.when(t == half - 9)
        def _():
            @pl.when(jnp.logical_not(first))
            def _():
                state_up.start()

            @pl.when(jnp.logical_not(last))
            def _():
                state_down.start()

        @pl.when(t == half - 2)
        def _():
            @pl.when(jnp.logical_not(last))
            def _():
                coef_up.wait_recv()
                state_up.wait_recv()

            @pl.when(jnp.logical_not(first))
            def _():
                coef_down.wait_recv()
                state_down.wait_recv()

            build(0)
            build(PAD + rows)

    lanes = lax.broadcasted_iota(jnp.int32, (members, 128), 1)
    wide = lax.broadcasted_iota(jnp.int32, (members, cols), 1)

    def gather(o, found):
        cell = lax.rem(cell_ref[0, o], rows * cols)
        row = lax.div(cell, cols)
        col = lax.rem(cell, cols)
        value = jnp.sum(jnp.where(wide == col, nw[row], 0.0), axis=1, keepdims=True)
        return jnp.where(lanes == o, value, found)

    found = lax.fori_loop(0, n_obs, gather, jnp.zeros((members, 128), jnp.float32), unroll=8)
    predicted = found[:, :n_obs]
    xall[me_ens] = jnp.concatenate(
        [predicted * inv_spread, (target - predicted) * inv_spread], axis=1)
    share_pred = remote(xall.at[me_ens], xall.at[me_ens], ens_send.at[1], ens_recv.at[1], {"ens": other})
    share_pred.start()

    finish(pairs - 1)
    share_pred.wait()
    total = members * n_ens
    norm_factor = 1.0 / math.sqrt(total - 1)
    everyone = jnp.concatenate([xall[e] for e in range(n_ens)], axis=0)
    scaled, misfit = everyone[:, :n_obs], everyone[:, n_obs:]
    anomaly = (scaled - jnp.mean(scaled, axis=0, keepdims=True)) * norm_factor
    here = me_tm * n_sp + me_sp
    right = jnp.concatenate(
        [anomaly, misfit, jnp.zeros((128 - 2 * total, n_obs), jnp.float32)], axis=0)
    sums[here] = lax.dot_general(anomaly, right, NT, precision=HIGH,
                                 preferred_element_type=jnp.float32)

    def sum_copy(slot, t, z):
        return remote(sums.at[slot], sums.at[slot], sum_send.at[t * n_sp + z], sum_recv.at[slot],
                      {"tm": t, "space": z})

    for t, z in chips:
        sum_copy(here, t, z).start()
    for t, z in chips:
        sum_copy(t * n_sp + z, t, z).wait_recv()
    system = jnp.sum(sums[...], axis=0)

    row_no = lax.broadcasted_iota(jnp.int32, (total, 128), 0)
    system = system + (row_no == lax.broadcasted_iota(jnp.int32, (total, 128), 1)).astype(jnp.float32)
    for k in range(total):
        pivot_row = system[k:k + 1, :] / system[k:k + 1, k:k + 1]
        system = jnp.where(row_no == k, pivot_row, system - system[:, k:k + 1] * pivot_row)
    weights = system[:, total:2 * total]

    share_params.wait()
    every_param = jnp.concatenate([pall[e] for e in range(n_ens)], axis=0)
    param_anom = every_param - jnp.mean(every_param, axis=0, keepdims=True)
    update = lax.dot_general(weights, param_anom, TN, precision=HIGH,
                             preferred_element_type=jnp.float32) * norm_factor
    own = jnp.where(me_ens == 0, update[:members], update[members:])
    new_params_ref[...] = params_ref[...] + own

    @pl.when(jnp.logical_not(first))
    def _():
        coef_up.wait_send()
        state_up.wait_send()

    @pl.when(jnp.logical_not(last))
    def _():
        coef_down.wait_send()
        state_down.wait_send()

    @pl.when(sends)
    def _():
        @pl.when(jnp.logical_not(first))
        def _():
            edge_up.wait_send()

        @pl.when(jnp.logical_not(last))
        def _():
            edge_down.wait_send()

        for row in (*range(AHEAD), *range(rows - AHEAD, rows)):
            row_copy(row).wait_send()

    for t, z in chips:
        sum_copy(here, t, z).wait_send()


def per_device(sizes, start_states, velocity_x, velocity_y, diffusivity, source_shape, params,
               obs_cell, obs_data, obs_noise, obs_var):
    state = start_states[0]
    members, rows, cols = state.shape
    n_tm, n_sp, n_ens = sizes
    total = members * n_ens
    padded = (rows + 2 * PAD, members, cols)
    f32 = jnp.float32
    vmem = pl.BlockSpec(memory_space=pltpu.VMEM)
    hbm = pl.BlockSpec(memory_space=pl.ANY)
    dma = pltpu.SemaphoreType.DMA
    pairs = rows // 16
    new_states, new_params = pl.pallas_call(
        functools.partial(kernel, sizes),
        out_shape=(jax.ShapeDtypeStruct(state.shape, f32), jax.ShapeDtypeStruct(params.shape, f32)),
        in_specs=[hbm] * 10,
        out_specs=(vmem, vmem),
        scratch_shapes=[
            pltpu.VMEM(state.shape, f32),
            pltpu.VMEM(params.shape, f32),
            pltpu.SMEM(obs_cell.shape, jnp.int32),
            pltpu.VMEM(obs_data.shape, f32),
            pltpu.VMEM((total, obs_data.shape[1]), f32),
            pltpu.VMEM(obs_var.shape, f32),
            pltpu.VMEM(padded, f32),
            pltpu.VMEM(padded, f32),
            pltpu.VMEM(padded, f32),
            pltpu.VMEM(padded, f32),
            pltpu.VMEM((rows, members, cols), f32),
            pltpu.VMEM((rows + 2, members, cols), f32),
            pltpu.VMEM((4, rows + 2 * PAD, cols), f32),
            pltpu.VMEM((rows + 2 * PAD, 6, members, cols), f32),
            pltpu.VMEM((members, cols), f32),
            pltpu.VMEM((n_ens,) + params.shape, f32),
            pltpu.VMEM((n_ens, members, 128), f32),
            pltpu.VMEM((n_tm * n_sp, total, 128), f32),
            dma((4,)), dma((5,)), dma((2, pairs)),
            dma((4,)), dma((4,)),
            dma((rows,)), dma((rows,)),
            dma((2,)), dma((2,)),
            dma((2,)), dma((2,)),
            dma((n_tm * n_sp,)), dma((n_tm * n_sp,)),
        ],
        compiler_params=pltpu.CompilerParams(
            collective_id=0, has_side_effects=True, vmem_limit_bytes=60 * 2**20
        ),
    )(state, velocity_x, velocity_y, diffusivity, source_shape, params,
      obs_cell, obs_data, jnp.swapaxes(obs_noise[0], 0, 1), obs_var)
    return (new_states[None], new_params)


def solution(mesh):
    sizes = tuple(mesh.shape[axis] for axis in ("tm", "space", "ens"))
    in_specs = (
        P("tm", "ens", "space", None),
        P("space", None),
        P("space", None),
        P("space", None),
        P("space", None),
        P("ens", None),
        P("tm", "space"),
        P("tm", "space"),
        P("tm", "space", None),
        P("tm", "space"),
    )
    out_specs = (P("tm", "ens", "space", None), P("ens", None))
    return jax.shard_map(
        functools.partial(per_device, sizes), mesh=mesh,
        in_specs=in_specs, out_specs=out_specs, check_vma=False,
    )
```

```python
import functools
import math

import jax
import jax.numpy as jnp
from jax import lax
from jax.experimental import pallas as pl
from jax.experimental.pallas import tpu as pltpu
from jax.sharding import PartitionSpec as P

FINE = 4
FINE_DT = 0.25
PAD = 8
AHEAD = 3
MESH = pl.DeviceIdType.MESH
HIGH = lax.Precision.HIGHEST
NT = (((1,), (1,)), ((), ()))
TN = (((0,), (0,)), ((), ()))


def kernel(
    sizes,
    start_hbm, vx_hbm, vy_hbm, diff_hbm, src_hbm, params_hbm,
    cell_hbm, data_hbm, noise_hbm, var_hbm,
    out_ref, new_params_ref,
    start_ref, params_ref, cell_ref, data_ref, noise_ref, var_ref,
    st, a1, a2, a3, nw, rv, craw, cf, par, pall, xall, sums,
    in_sem, small_sem, block_sem,
    halo_send, halo_recv, row_send, row_recv, edge_send, edge_recv,
    ens_send, ens_recv, sum_send, sum_recv,
):
    n_tm, n_sp, n_ens = sizes
    me_tm = lax.axis_index("tm")
    me_sp = lax.axis_index("space")
    me_ens = lax.axis_index("ens")
    members, rows, cols = start_ref.shape
    half = rows // 2
    pairs = half // 8
    bands = params_ref.shape[1]
    n_obs = data_ref.shape[1]
    other = 1 - me_ens
    first, last = me_sp == 0, me_sp == n_sp - 1
    up_sp = lax.rem(me_sp + n_sp - 1, n_sp)
    dn_sp = lax.rem(me_sp + 1, n_sp)
    next_tm = lax.rem(me_tm + 1, n_tm)
    sends = me_tm < n_tm - 1
    receives = me_tm > 0

    def block_of(pair, side):
        at = half - 8 - 8 * pair if side == 0 else half + 8 * pair
        return at if isinstance(pair, int) else pl.multiple_of(at, 8)

    def start_in(pair, side):
        at = pl.ds(block_of(pair, side), 8)
        return pltpu.make_async_copy(start_hbm.at[:, at], start_ref.at[:, at], block_sem.at[side, pair])

    def coef_in(k):
        ref = (diff_hbm, vx_hbm, vy_hbm, src_hbm)[k]
        return pltpu.make_async_copy(ref, craw.at[k, pl.ds(PAD, rows)], in_sem.at[k])

    small = [
        pltpu.make_async_copy(src, dst, small_sem.at[k])
        for k, (src, dst) in enumerate((
            (params_hbm, params_ref), (cell_hbm, cell_ref), (data_hbm, data_ref),
            (noise_hbm, noise_ref), (var_hbm, var_ref)))
    ]
    start_in(0, 0).start()
    start_in(0, 1).start()
    for k in range(4):
        coef_in(k).start()
    for copy in small:
        copy.start()
    for pair in range(1, pairs):
        start_in(pair, 0).start()
        start_in(pair, 1).start()

    barrier = pltpu.get_barrier_semaphore()
    chips = [(lax.rem(me_tm + t, n_tm), lax.rem(me_sp + z, n_sp))
             for t in range(n_tm) for z in range(n_sp) if t or z]
    greeted = [{"ens": other}] + [{"tm": t, "space": z} for t, z in chips]
    for device in greeted:
        pl.semaphore_signal(barrier, inc=1, device_id=device, device_id_type=MESH)

    def remote(src, dst, send, recv, device):
        return pltpu.make_async_remote_copy(
            src_ref=src, dst_ref=dst, send_sem=send, recv_sem=recv,
            device_id=device, device_id_type=MESH,
        )

    up = {"space": up_sp}
    down = {"space": dn_sp}
    coef_up = remote(craw.at[:, pl.ds(PAD, 8)], craw.at[:, pl.ds(PAD + rows, 8)],
                     halo_send.at[0], halo_recv.at[0], up)
    coef_down = remote(craw.at[:, pl.ds(PAD + rows - 8, 8)], craw.at[:, pl.ds(0, 8)],
                       halo_send.at[1], halo_recv.at[1], down)
    state_up = remote(st.at[pl.ds(PAD, FINE)], st.at[pl.ds(PAD + rows, FINE)],
                      halo_send.at[2], halo_recv.at[2], up)
    state_down = remote(st.at[pl.ds(PAD + rows - FINE, FINE)], st.at[pl.ds(PAD - FINE, FINE)],
                        halo_send.at[3], halo_recv.at[3], down)

    lane = lax.broadcasted_iota(jnp.int32, (8, cols), 1)

    def build(at):
        at = pl.ds(at, 8)
        d = craw[0, at, :] * FINE_DT
        hx = craw[1, at, :] * (0.5 * FINE_DT)
        hy = craw[2, at, :] * (0.5 * FINE_DT)
        parts = [
            -4.0 * d, d + hy, d - hy,
            jnp.where(lane == 0, 0.0, d + hx),
            jnp.where(lane == cols - 1, 0.0, d - hx),
            craw[3, at, :] * FINE_DT, d, d,
        ]
        cf[at] = jnp.swapaxes(jnp.stack(parts, axis=0), 0, 1)

    def prepare(pair):
        for side in (0, 1):
            start_in(pair, side).wait()
            at = block_of(pair, side)
            st[pl.ds(PAD + at, 8)] = jnp.swapaxes(start_ref[:, pl.ds(at, 8), :], 0, 1)
            build(PAD + at if isinstance(pair, int) else pl.multiple_of(PAD + at, 8))

    small[0].wait()
    pick = (lax.broadcasted_iota(jnp.int32, (bands, cols), 1) // (cols // bands)
            == lax.broadcasted_iota(jnp.int32, (bands, cols), 0)).astype(jnp.float32)
    par[...] = jnp.dot(params_ref[...], pick, precision=HIGH, preferred_element_type=jnp.float32)
    pall[me_ens] = params_ref[...]
    for k in range(4):
        coef_in(k).wait()
    prepare(0)

    @pl.when(first)
    def _():
        craw[:, 0:PAD, :] = jnp.zeros((4, PAD, cols), jnp.float32)
        st[0:PAD] = jnp.zeros((PAD, members, cols), jnp.float32)
        rv[0] = jnp.zeros((members, cols), jnp.float32)

    @pl.when(last)
    def _():
        craw[:, PAD + rows:, :] = jnp.zeros((4, PAD, cols), jnp.float32)
        st[PAD + rows:] = jnp.zeros((PAD, members, cols), jnp.float32)
        rv[rows + 1] = jnp.zeros((members, cols), jnp.float32)

    def spread(row, above, middle, below):
        c = [cf[row + PAD, k:k + 1, :] for k in range(5)]
        return (c[0] * middle + c[1] * above + c[2] * below
                + c[3] * pltpu.roll(middle, 1, 1) + c[4] * pltpu.roll(middle, cols - 1, 1))

    def fine(field, row):
        at = row + PAD
        middle = field[at]
        force = cf[at, 5:6, :] * par[...]
        return middle + (spread(row, field[at - 1], middle, field[at + 1]) + force)

    def coarse(row):
        above, middle, below = (rv[row + k] - st[row + PAD - 1 + k] for k in range(3))
        return middle + spread(row, above, middle, below) * float(FINE)

    def row_copy(row):
        return remote(nw.at[row], rv.at[row + 1], row_send.at[row], row_recv.at[row], {"tm": next_tm})

    edge_up = remote(nw.at[0], rv.at[rows + 1], edge_send.at[0], edge_recv.at[0],
                     {"tm": next_tm, "space": up_sp})
    edge_down = remote(nw.at[rows - 1], rv.at[0], edge_send.at[1], edge_recv.at[1],
                       {"tm": next_tm, "space": dn_sp})

    def both(away):
        return half - 1 - away, half + away

    def finish(pair):
        for side in (0, 1):
            at = block_of(pair, side)
            out_ref[:, pl.ds(at, 8), :] = jnp.swapaxes(nw[pl.ds(at, 8)], 0, 1)

    def fine_both(field, away):
        return [fine(field, row) for row in both(away)]

    def keep(field, away, values):
        for row, value in zip(both(away), values):
            field[row + PAD] = value

    fields = (st, a1, a2, a3)

    def fine_steps(t, count):
        for k in reversed(range(count)):
            keep(fields[k + 1], t - 2 * k, fine_both(fields[k], t - 2 * k))

    for count in range(1, FINE):
        @pl.loop(2 * count - 2, 2 * count)
        def _(t):
            fine_steps(t, count)

    pl.semaphore_wait(barrier, len(greeted))
    share_params = remote(params_ref, pall.at[me_ens], ens_send.at[0], ens_recv.at[0], {"ens": other})
    share_params.start()

    @pl.when(jnp.logical_not(first))
    def _():
        coef_up.start()

    @pl.when(jnp.logical_not(last))
    def _():
        coef_down.start()

    for copy in small[1:]:
        copy.wait()
    mine = (lax.broadcasted_iota(jnp.int32, (members, members * n_ens), 1)
            == lax.broadcasted_iota(jnp.int32, (members, members * n_ens), 0) + me_ens * members)
    noise = lax.dot_general(mine.astype(jnp.float32), noise_ref[...], (((1,), (0,)), ((), ())),
                            precision=HIGH, preferred_element_type=jnp.float32)
    target = data_ref[...] + noise
    inv_spread = lax.rsqrt(var_ref[...])

    delay = 2 * (FINE - 1)

    @pl.loop(delay, half + delay)
    def _(t):
        q = t - delay
        upper, lower = both(q)
        values = fine_both(a3, q)
        nw[upper] = values[0]
        nw[lower] = values[1]
        fine_steps(t, FINE - 1)

        @pl.when(receives)
        def _():
            @pl.when(q == 0)
            def _():
                row_copy(half - 1).wait_recv()
                row_copy(half).wait_recv()

            @pl.when(q < half - 1)
            def _():
                row_copy(upper - 1).wait_recv()
                row_copy(lower + 1).wait_recv()

            @pl.when(q == half - 1)
            def _():
                @pl.when(jnp.logical_not(last))
                def _():
                    edge_up.wait_recv()

                @pl.when(jnp.logical_not(first))
                def _():
                    edge_down.wait_recv()

            more = [coarse(upper), coarse(lower)]
            nw[upper] = nw[upper] + more[0]
            nw[lower] = nw[lower] + more[1]

        @pl.when(sends)
        def _():
            @pl.when(q == half - 1)
            def _():
                @pl.when(jnp.logical_not(first))
                def _():
                    edge_up.start()

                @pl.when(jnp.logical_not(last))
                def _():
                    edge_down.start()

            @pl.when(q >= AHEAD)
            def _():
                row_copy(upper + AHEAD).wait_send()
                row_copy(lower - AHEAD).wait_send()

            row_copy(upper).start()
            row_copy(lower).start()

        @pl.when(jnp.logical_and(lax.rem(q, 8) == 7, q < half - 1))
        def _():
            finish(q // 8)

        @pl.when(jnp.logical_and(lax.rem(t, 8) == 6, t < half - 2))
        def _():
            prepare((t + 2) // 8)

        @pl.when(t == half - 9)
        def _():
            @pl.when(jnp.logical_not(first))
            def _():
                state_up.start()

            @pl.when(jnp.logical_not(last))
            def _():
                state_down.start()

        @pl.when(t == half - 2)
        def _():
            @pl.when(jnp.logical_not(last))
            def _():
                coef_up.wait_recv()
                state_up.wait_recv()

            @pl.when(jnp.logical_not(first))
            def _():
                coef_down.wait_recv()
                state_down.wait_recv()

            build(0)
            build(PAD + rows)

    lanes = lax.broadcasted_iota(jnp.int32, (members, 128), 1)
    wide = lax.broadcasted_iota(jnp.int32, (members, cols), 1)

    def gather(o, found):
        cell = lax.rem(cell_ref[0, o], rows * cols)
        row = lax.div(cell, cols)
        col = lax.rem(cell, cols)
        value = jnp.sum(jnp.where(wide == col, nw[row], 0.0), axis=1, keepdims=True)
        return jnp.where(lanes == o, value, found)

    found = lax.fori_loop(0, n_obs, gather, jnp.zeros((members, 128), jnp.float32), unroll=8)
    predicted = found[:, :n_obs]
    xall[me_ens] = jnp.concatenate(
        [predicted * inv_spread, (target - predicted) * inv_spread], axis=1)
    share_pred = remote(xall.at[me_ens], xall.at[me_ens], ens_send.at[1], ens_recv.at[1], {"ens": other})
    share_pred.start()

    finish(pairs - 1)
    share_pred.wait()
    total = members * n_ens
    norm_factor = 1.0 / math.sqrt(total - 1)
    everyone = jnp.concatenate([xall[e] for e in range(n_ens)], axis=0)
    scaled, misfit = everyone[:, :n_obs], everyone[:, n_obs:]
    anomaly = (scaled - jnp.mean(scaled, axis=0, keepdims=True)) * norm_factor
    here = me_tm * n_sp + me_sp
    right = jnp.concatenate(
        [anomaly, misfit, jnp.zeros((128 - 2 * total, n_obs), jnp.float32)], axis=0)
    sums[here] = lax.dot_general(anomaly, right, NT, precision=HIGH,
                                 preferred_element_type=jnp.float32)

    def sum_copy(slot, t, z):
        return remote(sums.at[slot], sums.at[slot], sum_send.at[t * n_sp + z], sum_recv.at[slot],
                      {"tm": t, "space": z})

    for t, z in chips:
        sum_copy(here, t, z).start()
    for t, z in chips:
        sum_copy(t * n_sp + z, t, z).wait_recv()
    system = jnp.sum(sums[...], axis=0)

    row_no = lax.broadcasted_iota(jnp.int32, (total, 128), 0)
    system = system + (row_no == lax.broadcasted_iota(jnp.int32, (total, 128), 1)).astype(jnp.float32)
    for k in range(total):
        pivot_row = system[k:k + 1, :] / system[k:k + 1, k:k + 1]
        system = jnp.where(row_no == k, pivot_row, system - system[:, k:k + 1] * pivot_row)
    weights = system[:, total:2 * total]

    share_params.wait()
    every_param = jnp.concatenate([pall[e] for e in range(n_ens)], axis=0)
    param_anom = every_param - jnp.mean(every_param, axis=0, keepdims=True)
    update = lax.dot_general(weights, param_anom, TN, precision=HIGH,
                             preferred_element_type=jnp.float32) * norm_factor
    own = jnp.where(me_ens == 0, update[:members], update[members:])
    new_params_ref[...] = params_ref[...] + own

    @pl.when(jnp.logical_not(first))
    def _():
        coef_up.wait_send()
        state_up.wait_send()

    @pl.when(jnp.logical_not(last))
    def _():
        coef_down.wait_send()
        state_down.wait_send()

    @pl.when(sends)
    def _():
        @pl.when(jnp.logical_not(first))
        def _():
            edge_up.wait_send()

        @pl.when(jnp.logical_not(last))
        def _():
            edge_down.wait_send()

        for row in (*range(AHEAD), *range(rows - AHEAD, rows)):
            row_copy(row).wait_send()

    for t, z in chips:
        sum_copy(here, t, z).wait_send()


def hand_over(states_hbm, params_hbm, out_hbm, new_params_hbm, held, held_params, in_sem, out_sem):
    count = states_hbm.shape[0]
    pieces = [(states_hbm.at[k], held.at[k], out_hbm.at[k]) for k in range(count)]
    pieces.append((params_hbm, held_params, new_params_hbm))
    arriving = [pltpu.make_async_copy(src, mid, in_sem.at[k]) for k, (src, mid, _) in enumerate(pieces)]
    leaving = [pltpu.make_async_copy(mid, dst, out_sem.at[k]) for k, (_, mid, dst) in enumerate(pieces)]
    for copy in arriving:
        copy.start()
    for before, after in zip(arriving, leaving):
        before.wait()
        after.start()
    for copy in leaving:
        copy.wait()


def per_device(sizes, start_states, velocity_x, velocity_y, diffusivity, source_shape, params,
               obs_cell, obs_data, obs_noise, obs_var):
    state = start_states[0]
    members, rows, cols = state.shape
    n_tm, n_sp, n_ens = sizes
    total = members * n_ens
    padded = (rows + 2 * PAD, members, cols)
    f32 = jnp.float32
    vmem = pl.BlockSpec(memory_space=pltpu.VMEM)
    hbm = pl.BlockSpec(memory_space=pl.ANY)
    dma = pltpu.SemaphoreType.DMA
    pairs = rows // 16
    new_states, new_params = pl.pallas_call(
        functools.partial(kernel, sizes),
        out_shape=(jax.ShapeDtypeStruct(state.shape, f32), jax.ShapeDtypeStruct(params.shape, f32)),
        in_specs=[hbm] * 10,
        out_specs=(vmem, vmem),
        scratch_shapes=[
            pltpu.VMEM(state.shape, f32),
            pltpu.VMEM(params.shape, f32),
            pltpu.SMEM(obs_cell.shape, jnp.int32),
            pltpu.VMEM(obs_data.shape, f32),
            pltpu.VMEM((total, obs_data.shape[1]), f32),
            pltpu.VMEM(obs_var.shape, f32),
            pltpu.VMEM(padded, f32),
            pltpu.VMEM(padded, f32),
            pltpu.VMEM(padded, f32),
            pltpu.VMEM(padded, f32),
            pltpu.VMEM((rows, members, cols), f32),
            pltpu.VMEM((rows + 2, members, cols), f32),
            pltpu.VMEM((4, rows + 2 * PAD, cols), f32),
            pltpu.VMEM((rows + 2 * PAD, 8, cols), f32),
            pltpu.VMEM((members, cols), f32),
            pltpu.VMEM((n_ens,) + params.shape, f32),
            pltpu.VMEM((n_ens, members, 128), f32),
            pltpu.VMEM((n_tm * n_sp, total, 128), f32),
            dma((4,)), dma((5,)), dma((2, pairs)),
            dma((4,)), dma((4,)),
            dma((rows,)), dma((rows,)),
            dma((2,)), dma((2,)),
            dma((2,)), dma((2,)),
            dma((n_tm * n_sp,)), dma((n_tm * n_sp,)),
        ],
        compiler_params=pltpu.CompilerParams(
            collective_id=0, has_side_effects=True, vmem_limit_bytes=60 * 2**20
        ),
    )(state, velocity_x, velocity_y, diffusivity, source_shape, params,
      obs_cell, obs_data, jnp.swapaxes(obs_noise[0], 0, 1), obs_var)
    new_states, new_params = pl.pallas_call(
        hand_over,
        out_shape=(jax.ShapeDtypeStruct(state.shape, f32), jax.ShapeDtypeStruct(params.shape, f32)),
        in_specs=[hbm] * 2,
        out_specs=(hbm, hbm),
        scratch_shapes=[
            pltpu.VMEM(state.shape, f32), pltpu.VMEM(params.shape, f32),
            dma((members + 1,)), dma((members + 1,)),
        ],
        compiler_params=pltpu.CompilerParams(vmem_limit_bytes=60 * 2**20),
    )(new_states, new_params)
    return (new_states[None], new_params)


def solution(mesh):
    sizes = tuple(mesh.shape[axis] for axis in ("tm", "space", "ens"))
    in_specs = (
        P("tm", "ens", "space", None),
        P("space", None),
        P("space", None),
        P("space", None),
        P("space", None),
        P("ens", None),
        P("tm", "space"),
        P("tm", "space"),
        P("tm", "space", None),
        P("tm", "space"),
    )
    out_specs = (P("tm", "ens", "space", None), P("ens", None))
    return jax.shard_map(
        functools.partial(per_device, sizes), mesh=mesh,
        in_specs=in_specs, out_specs=out_specs, check_vma=False,
    )
```
